256 devices in a mesh: lat: 32 (over y, x, z_hi), lon: 4 (over z_lo), ens: 2 (over core).
Axes of the slice: x: 4, y: 4, z: 8 (z_hi: 2, z_lo: 4; z = z_hi * 4 + z_lo), core: 2. Of those that a mesh axis runs over, the one named last changes fastest.
Arguments:
- states: bfloat16 [2, 128, 1440, 256], P('ens', 'lat', 'lon'), may hold values from -6 to 6
- cotangent: bfloat16 [2, 128, 1440, 256], P('ens', 'lat', 'lon'), may hold values from -6 to 6
- kernels: bfloat16 [3, 128, 4, 7], replicated, may hold values from -1 to 1
- offsets: int32 [128], replicated, may hold values from -3 to 127, as said below
- mixing: bfloat16 [3, 2, 128, 128], replicated, may hold values from -0.3125 to 0.3125
- legendre: bfloat16 [384, 384, 128], P('lat'), may hold values from -0.5 to 0.5
- owner_order: int32 [384], replicated, may hold values from 0 to 383, each once
- spectral_gain: bfloat16 [384, 256], replicated, may hold values from -5 to 5
Outputs:
- next_state: bfloat16 [2, 128, 1440, 256], P('ens', 'lat', 'lon')
- grad_state: bfloat16 [2, 128, 1440, 256], P('ens', 'lat', 'lon')
- grad_mixing: float32 [3, 2, 128, 128], replicated
- grad_gain: float32 [384, 256], P(None, 'lon')
The draws below stay inside these ranges and needn't reach their ends.
Inputs may be any that keep to these rules, and one draw needn't show every extreme that they name: offsets[i] - i lies between -3 and 0. `owner_order`: every wavenumber 0 to 383 appears once.
All inputs are finite; a program needn't handle non-finite values.
Results may differ from the reference program's by a relative error of at most 0.01.
Values may be sent and summed in bfloat16 or wider, within the bound.
No kernel may reach another device: no remote copies, remote signals or barrier semaphores. Data moves between devices by JAX's collectives and lax.ppermute only.
A program may use at most 128 MiB of HBM per device.

```python
import math
import jax
import jax.numpy as jnp
from jax import lax

CHANNELS = 256
LONGITUDES = 1440
DEGREES = 384
BAND_REACH = 3
SUPPORT = 4
KERNELS = 3
GROUPS = 2
GROUP_WIDTH = 128
LATITUDES = 128
MEMBERS = 2


def draw_offsets(key, part):
    key = jax.random.fold_in(key, 11)
    shifts = jax.random.randint(key, (LATITUDES,), -BAND_REACH, BAND_REACH - SUPPORT + 2)
    latitudes = jnp.arange(LATITUDES, dtype=jnp.int32)
    shifts = jnp.where(latitudes == 0, -BAND_REACH, shifts)
    shifts = jnp.where(latitudes == LATITUDES - 1, BAND_REACH - SUPPORT + 1, shifts)
    return (latitudes + shifts).astype(jnp.int32)


def level_of(own_key, dims, cuts, least, top_value):
    factor_of = 1.0
    for dim, parts in cuts:
        draws = jax.random.uniform(jax.random.fold_in(jax.random.fold_in(own_key, 6), dim), (parts,), jnp.float32, least / len(cuts), top_value / len(cuts))
        factor_of = factor_of * jnp.repeat(jnp.exp(draws), dims[dim] // parts).reshape((-1,) + (1,) * (len(dims) - 1 - dim))
    return factor_of


def scatter_about(own_key, dims, scale, limit, split=(), held_as=jnp.bfloat16):
    loudness = level_of(own_key, dims, split, -0.22, 0.18) if split else 1.0
    values = jax.random.normal(own_key, dims, jnp.float32) * scale * loudness
    return jnp.minimum(jnp.maximum(values, -limit), limit).astype(held_as)


def setup_inputs(seed: int = 0) -> dict:
    seeds = jax.random.split(jax.random.key(seed), 9)
    return {
        "states": scatter_about(seeds[0], (MEMBERS, LATITUDES, LONGITUDES, CHANNELS), 1.0, 6.0, ((0, 2), (1, 32), (2, 4))),
        "cotangent": scatter_about(seeds[1], (MEMBERS, LATITUDES, LONGITUDES, CHANNELS), 1.0, 6.0, ((0, 2), (1, 32), (2, 4))),
        "kernels": scatter_about(seeds[2], (KERNELS, LATITUDES, SUPPORT, 2 * BAND_REACH + 1), (SUPPORT * (2 * BAND_REACH + 1)) ** -0.5, 1.0),
        "offsets": draw_offsets(jax.random.fold_in(seeds[8], 71), 0),
        "mixing": scatter_about(seeds[4], (KERNELS, GROUPS, GROUP_WIDTH, GROUP_WIDTH), (KERNELS * GROUP_WIDTH) ** -0.5, 0.3125),
        "legendre": scatter_about(seeds[5], (DEGREES, DEGREES, LATITUDES), LATITUDES ** -0.5, 0.5, ((0, 32),)),
        "owner_order": jax.random.permutation(seeds[6], DEGREES).astype(jnp.int32),
        "spectral_gain": scatter_about(seeds[7], (DEGREES, CHANNELS), 1.0, 5.0),
    }


highest = lax.Precision.HIGHEST
far_below = -1000000

def fourier_table(owner_order, points):
    longitudes = jnp.arange(points, dtype=jnp.int32)
    phases = longitudes[:, None] * owner_order[None, :] % points
    angles = phases.astype(jnp.float32) * (2.0 * math.pi / points)
    factor = 1.0 / math.sqrt(points)
    return jnp.stack([jnp.cos(angles) * factor, -jnp.sin(angles) * factor], axis=-1).astype(jnp.bfloat16)

def spectral(fields, wave_table, legendre, triangle, spectral_gain):
    table_wide = wave_table.astype(jnp.float32)
    analysed = jnp.einsum('tnc,nkr->tkrc', fields.astype(jnp.float32), table_wide, precision=highest).astype(jnp.bfloat16)
    legendre_wide = legendre.astype(jnp.float32)
    coeffs = jnp.einsum('klt,tkrc->klrc', legendre_wide, analysed.astype(jnp.float32), precision=highest)
    coeffs = coeffs * triangle[:, :, None, None]
    weighted_terms = (coeffs * spectral_gain.astype(jnp.float32)[None, :, None, :]).astype(jnp.bfloat16)
    synthesis = jnp.einsum('klt,klrc->ktrc', legendre_wide, weighted_terms.astype(jnp.float32), precision=highest).astype(jnp.bfloat16)
    spectrum = jnp.einsum('ktrc,nkr->tnc', synthesis.astype(jnp.float32), table_wide, precision=highest).astype(jnp.bfloat16)
    return (spectrum, coeffs)

def padded_field(fields):
    rows_padded = jnp.pad(fields, ((BAND_REACH, BAND_REACH), (0, 0), (0, 0)))
    return jnp.concatenate([rows_padded[:, LONGITUDES - BAND_REACH:], rows_padded, rows_padded[:, :BAND_REACH]], axis=1)

def band_row(whole_field, first_row, kernel_row):
    window = lax.dynamic_slice_in_dim(whole_field, first_row + BAND_REACH, SUPPORT, 0).astype(jnp.float32)
    running = jnp.zeros((KERNELS, LONGITUDES, CHANNELS), jnp.float32)
    for step_lon in range(2 * BAND_REACH + 1):
        running = running + jnp.einsum('bk,knc->bnc', kernel_row[:, :, step_lon].astype(jnp.float32), window[:, step_lon:step_lon + LONGITUDES], precision=highest)
    return running

def forward_mixing(fields, kernels, offsets, mixing):
    whole_field = padded_field(fields)
    mixing_wide = mixing.astype(jnp.float32)

    def one_row(running_sum, inputs):
        first_row, kernel_row = inputs
        basis_row = lax.optimization_barrier(band_row(whole_field, first_row, kernel_row).astype(jnp.bfloat16)).astype(jnp.float32)
        mixed_row = jnp.einsum('bngc,bgce->nge', basis_row.reshape(KERNELS, LONGITUDES, GROUPS, GROUP_WIDTH), mixing_wide, precision=highest)
        return (running_sum, mixed_row.reshape(LONGITUDES, CHANNELS))
    unused, mixed = lax.scan(one_row, jnp.zeros((), jnp.float32), (offsets, jnp.moveaxis(kernels, 1, 0)))
    return mixed

def mixing_weight_gradient(fields, grad_pre, kernels, offsets):
    whole_field = padded_field(fields)

    def one_row(running_sum, inputs):
        first_row, kernel_row, grad_row = inputs
        basis_row = lax.optimization_barrier(band_row(whole_field, first_row, kernel_row).astype(jnp.bfloat16)).astype(jnp.float32)
        product = jnp.einsum('bngc,nge->bgce', basis_row.reshape(KERNELS, LONGITUDES, GROUPS, GROUP_WIDTH), grad_row.astype(jnp.float32).reshape(LONGITUDES, GROUPS, GROUP_WIDTH), precision=highest)
        return (running_sum + product, None)
    start_sum = jnp.zeros((KERNELS, GROUPS, GROUP_WIDTH, GROUP_WIDTH), jnp.float32)
    grand_sum_value, unused = lax.scan(one_row, start_sum, (offsets, jnp.moveaxis(kernels, 1, 0), grad_pre))
    return grand_sum_value

def adjoint_mixing(grad_pre, kernels, offsets, mixing):
    whole_field = padded_field(grad_pre)
    kernels_pad = jnp.pad(kernels, ((0, 0), (BAND_REACH, BAND_REACH), (0, 0), (0, 0)))
    offsets_pad = jnp.pad(offsets, BAND_REACH, constant_values=far_below)
    reach_rows = 2 * BAND_REACH + 1
    support_index = jnp.arange(SUPPORT, dtype=jnp.int32)
    mixing_wide = mixing.astype(jnp.float32)

    def one_row(running_sum, row_index):
        near_starts = lax.dynamic_slice_in_dim(offsets_pad, row_index, reach_rows, 0)
        near_kernels = lax.dynamic_slice_in_dim(kernels_pad, row_index, reach_rows, 1).astype(jnp.float32)
        matches = ((row_index - near_starts)[:, None] == support_index[None, :]).astype(jnp.float32)
        coupling = jnp.einsum('bakd,ak->abd', near_kernels, matches, precision=highest)
        window = lax.dynamic_slice_in_dim(whole_field, row_index, reach_rows, 0).astype(jnp.float32)
        running = jnp.zeros((KERNELS, LONGITUDES, CHANNELS), jnp.float32)
        for step_lon in range(reach_rows):
            first_col = 2 * BAND_REACH - step_lon
            running = running + jnp.einsum('ab,anc->bnc', coupling[:, :, step_lon], window[:, first_col:first_col + LONGITUDES], precision=highest)
        spread_row = lax.optimization_barrier(running.astype(jnp.bfloat16)).astype(jnp.float32)
        backward_row = jnp.einsum('bnge,bgce->ngc', spread_row.reshape(KERNELS, LONGITUDES, GROUPS, GROUP_WIDTH), mixing_wide, precision=highest)
        return (running_sum, backward_row.reshape(LONGITUDES, CHANNELS))
    unused, backward = lax.scan(one_row, jnp.zeros((), jnp.float32), jnp.arange(LATITUDES, dtype=jnp.int32))
    return backward

def reference(states, cotangent, kernels, offsets, mixing, legendre, owner_order, spectral_gain):
    wave_table = fourier_table(owner_order, LONGITUDES)
    degree_index = jnp.arange(DEGREES, dtype=jnp.int32)
    triangle = (degree_index[None, :] >= owner_order[:, None]).astype(jnp.float32)
    next_list = []
    grad_list = []
    grad_mixing = jnp.zeros((KERNELS, GROUPS, GROUP_WIDTH, GROUP_WIDTH), jnp.float32)
    grad_gain = jnp.zeros((DEGREES, CHANNELS), jnp.float32)
    for member in range(MEMBERS):
        fields = states[member]
        spectrum, coeffs = spectral(fields, wave_table, legendre, triangle, spectral_gain)
        preact = spectrum.astype(jnp.float32) + forward_mixing(fields, kernels, offsets, mixing)
        activated, pullback = jax.vjp(jax.nn.gelu, preact)
        next_list.append((fields.astype(jnp.float32) + activated).astype(jnp.bfloat16))
        incoming = cotangent[member].astype(jnp.float32)
        grad_pre = pullback(incoming)[0].astype(jnp.bfloat16)
        spec_back, coeffs_back = spectral(grad_pre, wave_table, legendre, triangle, spectral_gain)
        backward = adjoint_mixing(grad_pre, kernels, offsets, mixing)
        grad_list.append((incoming + spec_back.astype(jnp.float32) + backward).astype(jnp.bfloat16))
        grad_mixing = grad_mixing + mixing_weight_gradient(fields, grad_pre, kernels, offsets)
        grad_gain = grad_gain + lax.optimization_barrier(jnp.sum(coeffs * coeffs_back, axis=(0, 2)))
    mix_scale = 1.0 / math.sqrt(MEMBERS * LATITUDES * LONGITUDES)
    gain_scale = 1.0 / math.sqrt(2 * MEMBERS * DEGREES)
    return (jnp.stack(next_list), jnp.stack(grad_list), grad_mixing * mix_scale, grad_gain * gain_scale)
```

```python
import math

import jax
import jax.numpy as jnp
from jax import lax
from jax.experimental import pallas as pl
from jax.experimental.pallas import tpu as pltpu
from jax.sharding import PartitionSpec as P

LONGITUDES = 1440
BAND_REACH = 3
SUPPORT = 4
HALF = 64
LANES = 128
BLOCK = 32
WINDOW = 48
CHUNK = 48

bf16 = jnp.bfloat16
f32 = jnp.float32
highest = lax.Precision.HIGHEST
far_below = -1000000


def call(kernel, out_shape, args, flops, scratch=(), smem=(), limit=24):
    moved = sum(a.size * a.dtype.itemsize for a in args)
    moved += sum(math.prod(o.shape) * o.dtype.itemsize for o in out_shape)
    specs = [
        pl.BlockSpec(memory_space=pltpu.SMEM if i in smem else pltpu.VMEM)
        for i in range(len(args))
    ]
    return pl.pallas_call(
        kernel,
        out_shape=out_shape,
        in_specs=specs,
        out_specs=[pl.BlockSpec(memory_space=pltpu.VMEM) for _ in out_shape],
        scratch_shapes=list(scratch),
        compiler_params=pltpu.CompilerParams(vmem_limit_bytes=limit * 1024 * 1024),
        cost_estimate=pl.CostEstimate(
            flops=int(flops), bytes_accessed=int(moved), transcendentals=0
        ),
    )(*args)


def dot(a, b):
    return lax.dot_general(a, b, (((1,), (0,)), ((), ())), preferred_element_type=f32)


def swap_pair(first, second):
    left = lax.broadcasted_iota(jnp.int32, first.shape, 1) < HALF
    low = jnp.where(left, first, pltpu.roll(second, HALF, 1))
    high = jnp.where(left, pltpu.roll(first, HALF, 1), second)
    return low, high


def chunks(rows):
    return [(first, min(CHUNK, rows - first)) for first in range(0, rows, CHUNK)]


def pieces(rows):
    for first, count in chunks(rows):
        for a in range(2):
            for v in range(2):
                yield pl.ds(first, count), a, v, pl.ds(a * LANES, LANES), pl.ds(v * LANES, LANES)


def pack_kernel(x_ref, out_ref):
    for rows, a, v, at, av in pieces(x_ref.shape[1]):
        low, high = swap_pair(
            x_ref[2 * a, rows, av].astype(f32), x_ref[2 * a + 1, rows, av].astype(f32)
        )
        out_ref[2 * v, rows, at] = low.astype(bf16)
        out_ref[2 * v + 1, rows, at] = high.astype(bf16)


def analysis_kernel(circle_ref, wave_ref, *rest):
    extra_ref = rest[0] if len(rest) == 3 else None
    out_ref, rows_ref = rest[-2:]
    waves = wave_ref.shape[1] // 2
    sums = []
    for r in range(2):
        total = dot(wave_ref[0, r * waves : (r + 1) * waves, :], circle_ref[0])
        for s in range(1, wave_ref.shape[0]):
            total += dot(wave_ref[s, r * waves : (r + 1) * waves, :], circle_ref[s])
        sums.append(total)
    for a in range(2):
        lanes = slice(a * LANES, (a + 1) * LANES)
        low, high = swap_pair(sums[0][:, lanes], sums[1][:, lanes])
        rows_ref[pl.ds(2 * a, waves, stride=4), :] = low
        rows_ref[pl.ds(2 * a + 1, waves, stride=4), :] = high
    peers = out_ref.shape[0]
    main = 4 * waves // peers
    out_ref[:, 0:main, :] = rows_ref[...].reshape(peers, main, LANES).astype(bf16)
    if extra_ref is not None:
        out_ref[:, main:, :] = extra_ref[...]


def legendre_steps(order_ref, rows_in_ref, leg_ref, leg_turned_ref, gain_ref, rows_out_ref, peers, use):
    owned, degrees = leg_ref.shape[0], leg_ref.shape[1]
    step = 4 * owned
    degree = lax.broadcasted_iota(jnp.int32, (degrees, LANES), 0)
    for k in range(owned):
        field = jnp.concatenate(
            [rows_in_ref[pl.ds(4 * k + t, peers, stride=step), :] for t in range(4)], axis=0
        ).astype(bf16)
        coeffs = dot(leg_ref[k], field)
        coeffs = jnp.where(degree >= order_ref[k], coeffs, 0.0)
        use(k, coeffs)
        weighted = (coeffs * gain_ref[...]).astype(bf16)
        synthesis = dot(leg_turned_ref[k], weighted)
        for t in range(4):
            rows_out_ref[pl.ds(4 * k + t, peers, stride=step), :] = synthesis[
                t * peers : (t + 1) * peers
            ]


def legendre_forward_kernel(
    order_ref, got_ref, leg_ref, leg_turned_ref, gain_ref, out_ref, coeffs_ref, rows_in_ref, rows_out_ref
):
    peers = got_ref.shape[0]
    main = rows_in_ref.shape[0] // peers
    rows_in_ref[...] = got_ref[...].astype(f32).reshape(peers * main, LANES)

    def use(k, coeffs):
        coeffs_ref[k] = coeffs

    legendre_steps(order_ref, rows_in_ref, leg_ref, leg_turned_ref, gain_ref, rows_out_ref, peers, use)
    out_ref[...] = rows_out_ref[...].reshape(peers, main, LANES).astype(bf16)


def legendre_backward_kernel(
    order_ref, got_ref, leg_ref, leg_turned_ref, gain_ref, coeffs_ref, out_ref, rows_in_ref, rows_out_ref, sum_ref
):
    peers = got_ref.shape[0]
    main = rows_in_ref.shape[0] // peers
    rows_in_ref[...] = got_ref[:, 0:main, :].astype(f32).reshape(peers * main, LANES)

    def use(k, coeffs):
        term = coeffs * coeffs_ref[k]
        if k == 0:
            sum_ref[...] = term
        else:
            sum_ref[...] += term

    legendre_steps(order_ref, rows_in_ref, leg_ref, leg_turned_ref, gain_ref, rows_out_ref, peers, use)
    out_ref[:, 0:main, :] = rows_out_ref[...].reshape(peers, main, LANES).astype(bf16)
    total = sum_ref[...]
    total = total + pltpu.roll(total, HALF, 1)
    half = total.shape[0] // 2
    left = lax.broadcasted_iota(jnp.int32, (half, LANES), 1) < HALF
    packed = jnp.where(left, total[:half], total[half:])
    high = packed.astype(bf16).astype(f32)
    low = packed - high
    used = half // 8
    both = jnp.concatenate([high.reshape(used, 8, LANES), low.reshape(used, 8, LANES)], axis=1)
    out_ref[0:used, main : main + 16, :] = both.astype(bf16)
    if used < peers:
        out_ref[used:peers, main : main + 16, :] = jnp.zeros((peers - used, 16, LANES), bf16)


def synthesis_kernel(got_ref, wave_ref, out_ref, rows_ref):
    waves = wave_ref.shape[2] // 2
    peers = got_ref.shape[0]
    main = 4 * waves // peers
    rows_ref[...] = got_ref[:, 0:main, :].astype(f32).reshape(4 * waves, LANES)
    low, high = [], []
    for a in range(2):
        lo, hi = swap_pair(
            rows_ref[pl.ds(2 * a, waves, stride=4), :], rows_ref[pl.ds(2 * a + 1, waves, stride=4), :]
        )
        low.append(lo)
        high.append(hi)
    spectrum = jnp.concatenate(
        [jnp.concatenate(low, axis=1), jnp.concatenate(high, axis=1)], axis=0
    ).astype(bf16)
    for s in range(wave_ref.shape[0]):
        out_ref[s] = dot(wave_ref[s], spectrum).astype(bf16)


def band_kernel(x_ref, toeplitz_ref, mix_ref, *outs):
    mixed_ref = outs[0]
    basis_ref = outs[1] if len(outs) > 1 else None
    kernels = mix_ref.shape[0]
    span, channels = x_ref.shape[0], x_ref.shape[2]
    per_kernel = toeplitz_ref.shape[0] // kernels
    rows = per_kernel // BLOCK

    def step(j, carry):
        start = pl.multiple_of(j * BLOCK, BLOCK)
        window = x_ref[:, pl.ds(start, WINDOW), :].reshape(span * WINDOW, channels)
        basis = dot(toeplitz_ref[...], window).astype(bf16)
        total = None
        for b in range(kernels):
            part = basis[b * per_kernel : (b + 1) * per_kernel]
            if basis_ref is not None:
                basis_ref[b, :, pl.ds(start, BLOCK), :] = part.reshape(rows, BLOCK, channels)
            term = dot(part, mix_ref[b])
            total = term if total is None else total + term
        mixed_ref[:, pl.ds(start, BLOCK), :] = total.reshape(rows, BLOCK, channels)
        return carry

    lax.fori_loop(0, mixed_ref.shape[1] // BLOCK, step, 0)


def activation_kernel(
    spec_ref, mixed_ref, state_ref, cot_ref, next_ref, grad_ref, packed_ref
):
    scale = math.sqrt(2.0 / math.pi)
    for rows, a, v, at, av in pieces(state_ref.shape[1]):
        spectra = swap_pair(spec_ref[2 * v, rows, at].astype(f32), spec_ref[2 * v + 1, rows, at].astype(f32))
        grads = []
        for h in range(2):
            t = 2 * a + h
            value = spectra[h] + mixed_ref[t, rows, av]
            square = value * value
            turn = jnp.tanh(scale * value * (1.0 + 0.044715 * square))
            share = 0.5 + 0.5 * turn
            next_ref[t, rows, av] = (state_ref[t, rows, av].astype(f32) + value * share).astype(bf16)
            slope = share + (0.5 * scale) * value * (1.0 - turn * turn) * (1.0 + (3.0 * 0.044715) * square)
            grad = cot_ref[t, rows, av].astype(f32) * slope
            grad_ref[t, rows, av] = grad.astype(bf16)
            grads.append(grad)
        low, high = swap_pair(*grads)
        packed_ref[2 * v, rows, at] = low.astype(bf16)
        packed_ref[2 * v + 1, rows, at] = high.astype(bf16)


def finish_kernel(spec_ref, back_ref, cot_ref, out_ref):
    for rows, a, v, at, av in pieces(cot_ref.shape[1]):
        spectra = swap_pair(spec_ref[2 * v, rows, at].astype(f32), spec_ref[2 * v + 1, rows, at].astype(f32))
        for h in range(2):
            t = 2 * a + h
            out_ref[t, rows, av] = (
                cot_ref[t, rows, av].astype(f32) + spectra[h] + back_ref[t, rows, av]
            ).astype(bf16)


def mixing_gradient_kernel(basis_ref, grad_ref, out_ref):
    kernels, lat_rows = basis_ref.shape[0], basis_ref.shape[1]
    sector = grad_ref.shape[1]
    for g in range(2):
        lanes = pl.ds(g * LANES, LANES)
        totals = [None] * kernels
        for i in range(lat_rows):
            turned = grad_ref[i, :, lanes].astype(f32).T.astype(bf16)
            for b in range(kernels):
                term = dot(turned, basis_ref[b, i, 0:sector, lanes])
                totals[b] = term if totals[b] is None else totals[b] + term
        for b in range(kernels):
            out_ref[g, b] = totals[b].T


def wave_tables(owner_order, sector, sectors):
    factor = 1.0 / math.sqrt(LONGITUDES)
    n = jnp.arange(sector, dtype=jnp.int32)

    def table(phases, orders, axis):
        angles = (phases % LONGITUDES).astype(f32) * (2.0 * math.pi / LONGITUDES)
        c = jnp.cos(angles) * factor
        s = jnp.sin(angles) * factor
        c, s = lax.optimization_barrier((c, s))
        out = []
        for part in range(sectors):
            turns = (orders * part) % 4
            swap = turns % 2 == 1
            flip_c = jnp.where((turns == 1) | (turns == 2), -1.0, 1.0)
            flip_s = jnp.where((turns == 0) | (turns == 1), -1.0, 1.0)
            cos_part = jnp.where(swap, s, c) * flip_c
            sin_part = jnp.where(swap, c, s) * flip_s
            out.append(jnp.concatenate([cos_part, sin_part], axis=axis))
        return jnp.stack(out).astype(bf16)

    by_wave = table(owner_order[:, None] * n[None, :], owner_order[:, None], 0)
    by_point = table(n[:, None] * owner_order[None, :], owner_order[None, :], 1)
    return by_wave, by_point


def band_table(kernels_pad, offsets_pad, first_in, count_in, first_out, output_count):
    rows_kern = lax.dynamic_slice_in_dim(kernels_pad, first_in + BAND_REACH, count_in, 1)
    rows_start = lax.dynamic_slice_in_dim(offsets_pad, first_in + BAND_REACH, count_in, 0)
    targets = first_out + jnp.arange(output_count, dtype=jnp.int32)
    support_index = jnp.arange(SUPPORT, dtype=jnp.int32)
    matches = (
        rows_start[:, None, None] + support_index[None, :, None] == targets[None, None, :]
    ).astype(f32)
    return jnp.einsum("bikd,ikr->ibrd", rows_kern.astype(f32), matches, precision=highest)


def toeplitz(table, taps_turned):
    b, o, r, d = table.shape
    if taps_turned:
        table = table[..., ::-1]
    n = jnp.arange(BLOCK, dtype=jnp.int32)
    m = jnp.arange(WINDOW, dtype=jnp.int32)
    tap = m[None, :] - n[:, None]
    spread = (tap[None] == jnp.arange(d, dtype=jnp.int32)[:, None, None]).astype(bf16)
    out = jnp.einsum("bord,dnm->bonrm", table.astype(bf16), spread, preferred_element_type=f32)
    return out.astype(bf16).reshape(b * o * BLOCK, r * WINDOW)


def exchange(x, axis):
    return lax.all_to_all(x, axis, split_axis=0, concat_axis=0, tiled=True)


def with_columns(x):
    peers = lax.axis_size("lon")
    width = x.shape[1]
    up = [(i, (i + 1) % peers) for i in range(peers)]
    down = [(j, i) for i, j in up]
    before = lax.ppermute(x[:, width - BAND_REACH :], "lon", up)
    after = lax.ppermute(x[:, :BAND_REACH], "lon", down)
    return jnp.concatenate([before, x, after], axis=1)


def with_rows(x, even, width):
    peers = lax.axis_size("lat")
    pair = [(i, i ^ 1) for i in range(peers)]
    relay = [(i, (i + 2) % peers if i % 2 == 0 else (i - 2) % peers) for i in range(peers)]
    reach = BAND_REACH
    far = lax.ppermute(jnp.where(even, x[:reach], x[1 : reach + 1]), "lat", pair)
    rest = lax.ppermute(jnp.where(even, x[reach:], x[:1]), "lat", pair)
    other = lax.ppermute(far, "lat", relay)
    near = jnp.where(
        even, jnp.concatenate([rest, far[: reach - 1]]), jnp.concatenate([far[1:], rest])
    )
    before = jnp.where(even, other, near)
    after = jnp.where(even, near, other)
    whole = jnp.concatenate([before, x, after], axis=0)
    return jnp.pad(whole, ((0, 0), (0, width - whole.shape[1]), (0, 0)))


def on_device(states, cotangent, kernels, offsets, mixing, legendre, owner_order, spectral_gain):
    fields = states[0]
    cot = cotangent[0]
    lat_rows, sector, channels = fields.shape
    lon_index = lax.axis_index("lon")
    lat_index = lax.axis_index("lat")
    ens_index = lax.axis_index("ens")
    lon_count = lax.axis_size("lon")
    lat_count = lax.axis_size("lat")
    members = states.shape[0] * lax.axis_size("ens")
    lat_first = lat_index * lat_rows
    lat_total = lat_rows * lat_count
    extent = lat_rows + 2 * BAND_REACH
    kernel_number, group_count, width = mixing.shape[0], mixing.shape[1], mixing.shape[2]
    quarter = channels // lon_count
    owned, degrees = legendre.shape[0], legendre.shape[1]
    waves = owner_order.shape[0]
    main = 4 * owned
    even = lat_index % 2 == 0
    blocks = -(-sector // BLOCK)
    padded = blocks * BLOCK
    padded_in = padded + WINDOW - BLOCK
    sds = jax.ShapeDtypeStruct
    field_shape = sds((lat_rows, sector, channels), bf16)
    wide_shape = sds((lat_rows, padded, channels), f32)

    by_wave, by_point = wave_tables(owner_order, sector, lon_count)
    orders = lax.dynamic_slice_in_dim(owner_order, lat_index * owned, owned, 0)
    gains = lax.dynamic_slice_in_dim(spectral_gain, lon_index * quarter, quarter, 1).astype(f32)
    gains = jnp.concatenate([gains, gains], axis=1)
    leg = legendre.reshape(owned, degrees, lat_count, lat_rows)
    leg = jnp.swapaxes(leg, 2, 3).reshape(owned, degrees, lat_total)
    leg_turned = jnp.swapaxes(leg, 1, 2)
    kernels_pad = jnp.pad(kernels, ((0, 0), (BAND_REACH, BAND_REACH), (0, 0), (0, 0)))
    offsets_pad = jnp.pad(offsets, BAND_REACH, constant_values=far_below)
    forward_band = band_table(
        kernels_pad, offsets_pad, lat_first, lat_rows, lat_first - BAND_REACH, extent
    )
    rows_global = lat_first - BAND_REACH + jnp.arange(extent, dtype=jnp.int32)
    inside = (rows_global >= 0) & (rows_global < lat_total)
    forward_band = jnp.where(inside[None, None, :, None], forward_band, 0.0)
    backward_band = band_table(
        kernels_pad, offsets_pad, lat_first - BAND_REACH, extent, lat_first, lat_rows
    )
    forward_matrix = toeplitz(jnp.transpose(forward_band, (1, 0, 2, 3)), False)
    backward_matrix = toeplitz(jnp.transpose(backward_band, (1, 2, 0, 3)), True)
    groups = jnp.eye(group_count, dtype=bf16)
    mix_wide = (mixing[:, :, :, None, :] * groups[None, :, None, :, None]).reshape(
        kernel_number, channels, channels
    )
    mix_turned = jnp.swapaxes(mix_wide, 1, 2)

    transform_flops = 4 * waves * LONGITUDES * lat_rows * quarter
    legendre_flops = 4 * owned * degrees * lat_total * 2 * quarter
    band_flops = 2 * blocks * forward_matrix.size * channels
    row_scratch = pltpu.VMEM((4 * waves, LANES), f32)

    def band(x, matrix, mix, with_basis):
        outs = [wide_shape]
        if with_basis:
            outs.append(sds((kernel_number, lat_rows, padded, channels), bf16))
        return call(band_kernel, outs, (x, matrix, mix), band_flops)

    (packed,) = call(pack_kernel, [field_shape], (fields,), 0)
    circle = exchange(packed, "lon")
    extended = with_columns(fields)
    circle, extended = lax.optimization_barrier((circle, extended))
    (analysed,) = call(
        analysis_kernel,
        [sds((lat_count, main, LANES), bf16)],
        (circle, by_wave),
        transform_flops,
        [row_scratch],
    )
    owned_rows = exchange(analysed, "lat")
    x_padded = with_rows(extended, even, padded_in)
    synthesis, coeffs = call(
        legendre_forward_kernel,
        [sds((lat_count, main, LANES), bf16), sds((owned, degrees, LANES), f32)],
        (orders, owned_rows, leg, leg_turned, gains),
        legendre_flops,
        [row_scratch, row_scratch],
        (0,),
    )
    returned = exchange(synthesis, "lat")
    (spectrum,) = call(
        synthesis_kernel, [sds((lon_count, sector, channels), bf16)], (returned, by_point), transform_flops, [row_scratch]
    )
    spectrum = exchange(spectrum, "lon")
    mixed, basis = band(x_padded, forward_matrix, mix_wide, True)
    next_state, grad_pre, packed_back = call(
        activation_kernel,
        [field_shape, field_shape, field_shape],
        (spectrum, mixed, fields, cot),
        40 * fields.size,
    )

    circle_back = exchange(packed_back, "lon")
    extended_back = with_columns(grad_pre)
    (mix_part,) = call(
        mixing_gradient_kernel,
        [sds((group_count, kernel_number, width, width), f32)],
        (basis, grad_pre),
        2 * kernel_number * fields.size * width,
    )
    mix_part = mix_part.reshape(group_count, kernel_number * width, width)
    swap = [(0, 1), (1, 0)]
    kept = lax.dynamic_index_in_dim(mix_part, ens_index, 0, False)
    sent = lax.dynamic_index_in_dim(mix_part, 1 - ens_index, 0, False)
    mix_half = kept + lax.ppermute(sent, "ens", swap)
    mix_rows = mix_half.shape[0] // lat_count
    mix_high = lax.reduce_precision(mix_half, 8, 7)
    mix_chunks = jnp.concatenate(
        [
            mix_high.reshape(lat_count, mix_rows, width),
            (mix_half - mix_high).reshape(lat_count, mix_rows, width),
        ],
        axis=1,
    ).astype(bf16)
    circle_back, extended_back = lax.optimization_barrier((circle_back, extended_back))
    (analysed_back,) = call(
        analysis_kernel,
        [sds((lat_count, main + 2 * mix_rows, LANES), bf16)],
        (circle_back, by_wave, mix_chunks),
        transform_flops,
        [row_scratch],
    )
    owned_back = exchange(analysed_back, "lat")
    g_padded = with_rows(extended_back, even, padded_in)
    (synthesis_back,) = call(
        legendre_backward_kernel,
        [sds((lat_count, main + 16, LANES), bf16)],
        (orders, owned_back, leg, leg_turned, gains, coeffs),
        legendre_flops,
        [row_scratch, row_scratch, pltpu.VMEM((degrees, LANES), f32)],
        (0,),
    )
    mix_got = jnp.sum(owned_back[:, main:].astype(f32), axis=0)
    mix_got = lax.psum(mix_got[:mix_rows] + mix_got[mix_rows:], "lon")
    returned_back = exchange(synthesis_back, "lat")
    (spectrum_back,) = call(
        synthesis_kernel, [sds((lon_count, sector, channels), bf16)], (returned_back, by_point), transform_flops, [row_scratch]
    )
    gain_got = jnp.sum(returned_back[:, main:].astype(f32), axis=0)
    gain_got = gain_got[:8] + gain_got[8:]
    spectrum_back = exchange(spectrum_back, "lon")
    (backward,) = band(g_padded, backward_matrix, mix_turned, False)
    (grad_state,) = call(
        finish_kernel, [field_shape], (spectrum_back, backward, cot), 4 * fields.size
    )

    mix_scale = 1.0 / math.sqrt(members * lat_total * LONGITUDES)
    gain_scale = 1.0 / math.sqrt(2 * members * degrees)
    pieces_here = jnp.concatenate([gain_got, mix_got], axis=0)
    pieces_all = lax.all_gather(pieces_here, "lat", axis=0)
    gain_half = pieces_all[: degrees // 16, :8].reshape(degrees // 2, LANES)
    mix_mine = pieces_all[:, 8:].reshape(kernel_number * width, width)
    both = jnp.concatenate([gain_half, mix_mine], axis=0)
    other = lax.ppermute(both, "ens", swap)
    gain_sum = (gain_half + other[: degrees // 2]) * gain_scale
    grad_gain = jnp.concatenate([gain_sum[:, :quarter], gain_sum[:, quarter:]], axis=0)
    mix_other = other[degrees // 2 :]
    first = ens_index == 0
    mix_all = jnp.stack([jnp.where(first, mix_mine, mix_other), jnp.where(first, mix_other, mix_mine)])
    mix_all = mix_all.reshape(group_count, kernel_number, width, width) * mix_scale
    grad_mixing = jnp.swapaxes(mix_all, 0, 1)
    return (next_state[None], grad_state[None], grad_mixing, grad_gain)


def solution(mesh):
    in_specs = (
        P("ens", "lat", "lon", None),
        P("ens", "lat", "lon", None),
        P(),
        P(),
        P(),
        P("lat", None, None),
        P(),
        P(),
    )
    out_specs = (P("ens", "lat", "lon", None), P("ens", "lat", "lon", None), P(), P(None, "lon"))
    return jax.shard_map(
        on_device, mesh=mesh, in_specs=in_specs, out_specs=out_specs, check_vma=False
    )
```

```python
import functools
import math

import jax
import jax.numpy as jnp
from jax import lax
from jax.experimental import pallas as pl
from jax.experimental.pallas import tpu as pltpu
from jax.sharding import PartitionSpec as P

LONGITUDES = 1440
BAND_REACH = 3
SUPPORT = 4
HALF = 64
LANES = 128
BLOCK = 32
WINDOW = 48
CHUNK = 48
TILE = 96
WINDOWS = 3
EDGE = 16
PARTS = 3

bf16 = jnp.bfloat16
f32 = jnp.float32
highest = lax.Precision.HIGHEST
far_below = -1000000


VMEM = pltpu.VMEM
SMEM = pltpu.SMEM


def call(kernel, out_shape, args, flops, scratch=(), places=None, grid=(), blocks=None, outs=None, limit=24):
    moved = sum(a.size * a.dtype.itemsize for a in args)
    moved += sum(math.prod(o.shape) * jnp.dtype(o.dtype).itemsize for o in out_shape)
    places = places or {}
    specs = blocks or [pl.BlockSpec(memory_space=places.get(i, VMEM)) for i in range(len(args))]
    out_specs = outs or [
        pl.BlockSpec(memory_space=places[-1 - i]) if -1 - i in places else pl.BlockSpec()
        for i in range(len(out_shape))
    ]
    return pl.pallas_call(
        kernel,
        grid=grid,
        out_shape=out_shape,
        in_specs=specs,
        out_specs=out_specs,
        scratch_shapes=list(scratch),
        compiler_params=pltpu.CompilerParams(vmem_limit_bytes=limit * 1024 * 1024),
        cost_estimate=pl.CostEstimate(
            flops=int(flops), bytes_accessed=int(moved), transcendentals=0
        ),
    )(*args)


def hbm(x):
    return pltpu.with_memory_space_constraint(x, pltpu.HBM)


def dot(a, b):
    return lax.dot_general(a, b, (((1,), (0,)), ((), ())), preferred_element_type=f32)


def swap_pair(first, second):
    left = lax.broadcasted_iota(jnp.int32, first.shape, 1) < HALF
    low = jnp.where(left, first, pltpu.roll(second, HALF, 1))
    high = jnp.where(left, pltpu.roll(first, HALF, 1), second)
    return low, high


def quads():
    for a in range(2):
        for v in range(2):
            yield a, v, pl.ds(a * LANES, LANES), pl.ds(v * LANES, LANES)


def edge_rows(columns):
    rows = []
    for column in columns:
        rows += [column, jnp.zeros((1, column.shape[1]), f32)]
    return jnp.concatenate(rows, axis=0)


def pack_kernel(place_ref, x_ref, out_ref):
    sector = x_ref.shape[1]
    for first in range(0, sector, CHUNK):
        rows = pl.ds(first, min(CHUNK, sector - first))
        for a, v, at, av in quads():
            low, high = swap_pair(
                x_ref[2 * a, rows, av].astype(f32), x_ref[2 * a + 1, rows, av].astype(f32)
            )
            out_ref[2 * v, rows, at] = low.astype(bf16)
            out_ref[2 * v + 1, rows, at] = high.astype(bf16)
    lat_rows = x_ref.shape[0]
    begin = edge_rows([x_ref[t, 0:16, :].astype(f32)[:BAND_REACH] for t in range(lat_rows)])
    end = edge_rows([x_ref[t, sector - 8 : sector, :].astype(f32)[8 - BAND_REACH :] for t in range(lat_rows)])
    peers = out_ref.shape[0]
    for p in range(peers):
        to_right = p == lax.rem(place_ref[0] + 1, peers)
        out_ref[p, sector : sector + EDGE, :] = jnp.where(to_right, end, begin).astype(bf16)


def analysis_kernel(circle_ref, wave_ref, *rest):
    out_ref, rows_ref = rest[2:4] if len(rest) > 2 else rest
    copies = []
    if len(rest) > 2:
        terms_ref, sems = rest[4:]
        for j in range(2):
            copies.append(pltpu.make_async_copy(rest[j], terms_ref.at[j], sems.at[j]))
            copies[j].start()
    waves, sector = wave_ref.shape[1] // 2, wave_ref.shape[2]
    sums = []
    for r in range(2):
        total = None
        for s in range(wave_ref.shape[0]):
            term = dot(wave_ref[s, r * waves : (r + 1) * waves, :], circle_ref[s, 0:sector, :])
            total = term if total is None else total + term
        sums.append(total)
    for a in range(2):
        lanes = slice(a * LANES, (a + 1) * LANES)
        low, high = swap_pair(sums[0][:, lanes], sums[1][:, lanes])
        rows_ref[pl.ds(2 * a, waves, stride=4), :] = low
        rows_ref[pl.ds(2 * a + 1, waves, stride=4), :] = high
    peers = out_ref.shape[0]
    main = 4 * waves // peers
    out_ref[:, 0:main, :] = rows_ref[...].reshape(peers, main, LANES).astype(bf16)
    if copies:
        for copy in copies:
            copy.wait()
        out_ref[:, main:, :] = split_chunks(terms_ref[0] + terms_ref[1], peers)


def chunk_size(rows, peers):
    return 8 * -(-rows // (8 * peers))


def split_chunks(total, peers):
    high = total.astype(bf16).astype(f32)
    low = total - high
    size = chunk_size(total.shape[0], peers)
    used = total.shape[0] // size
    both = jnp.concatenate(
        [high.reshape(used, size, LANES), low.reshape(used, size, LANES)], axis=1
    )
    if used < peers:
        both = jnp.concatenate([both, jnp.zeros((peers - used, 2 * size, LANES), f32)], axis=0)
    return both.astype(bf16)


def joined(got):
    total = jnp.sum(got.astype(f32), axis=0)
    size = total.shape[0] // 2
    return total[:size] + total[size:]


def legendre_steps(order_ref, rows_in_ref, leg_ref, leg_turned_ref, gain_ref, rows_out_ref, peers, part, use):
    owned, degrees = leg_ref.shape[0], leg_ref.shape[1]
    step = 4 * owned
    degree = lax.broadcasted_iota(jnp.int32, (degrees, LANES), 0)
    for k in part:
        field = jnp.concatenate(
            [rows_in_ref[pl.ds(4 * k + t, peers, stride=step), :] for t in range(4)], axis=0
        ).astype(bf16)
        coeffs = dot(leg_ref[k], field)
        coeffs = jnp.where(degree >= order_ref[k], coeffs, 0.0)
        use(k, coeffs)
        weighted = (coeffs * gain_ref[...]).astype(bf16)
        synthesis = dot(leg_turned_ref[k], weighted)
        for t in range(4):
            rows_out_ref[pl.ds(4 * k + t, peers, stride=step), :] = synthesis[
                t * peers : (t + 1) * peers
            ]


def parts(owned):
    count = owned // PARTS
    return [(p, pl.ds(p * count, count), range(p * count, (p + 1) * count)) for p in range(PARTS)]


def legendre_forward_kernel(
    order_ref,
    got_ref,
    leg_hbm,
    leg_turned_hbm,
    gain_ref,
    out_ref,
    coeffs_hbm,
    rows_in_ref,
    rows_out_ref,
    held_ref,
    leg_ref,
    leg_turned_ref,
    sems,
):
    peers = got_ref.shape[0]
    main = rows_in_ref.shape[0] // peers
    reads, writes = [], []
    for p, at, _ in parts(leg_ref.shape[0]):
        reads.append(
            [
                pltpu.make_async_copy(leg_hbm.at[at], leg_ref.at[at], sems.at[0, p]),
                pltpu.make_async_copy(leg_turned_hbm.at[at], leg_turned_ref.at[at], sems.at[1, p]),
            ]
        )
        for copy in reads[p]:
            copy.start()
    rows_in_ref[...] = got_ref[...].astype(f32).reshape(peers * main, LANES)

    def use(k, coeffs):
        held_ref[k] = coeffs

    for p, at, part in parts(leg_ref.shape[0]):
        for copy in reads[p]:
            copy.wait()
        legendre_steps(
            order_ref, rows_in_ref, leg_ref, leg_turned_ref, gain_ref, rows_out_ref, peers, part, use
        )
        writes.append(pltpu.make_async_copy(held_ref.at[at], coeffs_hbm.at[at], sems.at[2, p]))
        writes[p].start()
    out_ref[...] = rows_out_ref[...].reshape(peers, main, LANES).astype(bf16)
    for copy in writes:
        copy.wait()


def legendre_backward_kernel(
    order_ref,
    got_ref,
    leg_hbm,
    leg_turned_hbm,
    gain_ref,
    coeffs_hbm,
    out_ref,
    mix_ref,
    rows_in_ref,
    rows_out_ref,
    sum_ref,
    held_ref,
    leg_ref,
    leg_turned_ref,
    sems,
):
    peers = got_ref.shape[0]
    main = rows_in_ref.shape[0] // peers
    reads = []
    for p, at, _ in parts(leg_ref.shape[0]):
        reads.append(
            [
                pltpu.make_async_copy(leg_hbm.at[at], leg_ref.at[at], sems.at[0, p]),
                pltpu.make_async_copy(leg_turned_hbm.at[at], leg_turned_ref.at[at], sems.at[1, p]),
                pltpu.make_async_copy(coeffs_hbm.at[at], held_ref.at[at], sems.at[2, p]),
            ]
        )
        for copy in reads[p]:
            copy.start()
    rows_in_ref[...] = got_ref[:, 0:main, :].astype(f32).reshape(peers * main, LANES)
    mix_ref[...] = joined(got_ref[:, main:, :])

    def use(k, coeffs):
        term = coeffs * held_ref[k]
        if k == 0:
            sum_ref[...] = term
        else:
            sum_ref[...] += term

    for p, _, part in parts(leg_ref.shape[0]):
        for copy in reads[p]:
            copy.wait()
        legendre_steps(
            order_ref, rows_in_ref, leg_ref, leg_turned_ref, gain_ref, rows_out_ref, peers, part, use
        )
    out_ref[:, 0:main, :] = rows_out_ref[...].reshape(peers, main, LANES).astype(bf16)
    total = sum_ref[...]
    total = total + pltpu.roll(total, HALF, 1)
    half = total.shape[0] // 2
    left = lax.broadcasted_iota(jnp.int32, (half, LANES), 1) < HALF
    out_ref[:, main:, :] = split_chunks(jnp.where(left, total[:half], total[half:]), peers)


def spectrum_of(got_ref, rows_ref, waves):
    peers = got_ref.shape[0]
    main = 4 * waves // peers
    rows_ref[...] = got_ref[:, 0:main, :].astype(f32).reshape(4 * waves, LANES)
    low, high = [], []
    for a in range(2):
        lo, hi = swap_pair(
            rows_ref[pl.ds(2 * a, waves, stride=4), :], rows_ref[pl.ds(2 * a + 1, waves, stride=4), :]
        )
        low.append(lo)
        high.append(hi)
    return jnp.concatenate(
        [jnp.concatenate(low, axis=1), jnp.concatenate(high, axis=1)], axis=0
    ).astype(bf16)


def synthesis_kernel(got_ref, wave_hbm, out_ref, rows_ref, wave_ref, sems):
    peers = out_ref.shape[0]
    reads = []
    for j in range(peers):
        reads.append(pltpu.make_async_copy(wave_hbm.at[j], wave_ref.at[j], sems.at[j]))
        reads[j].start()
    spectrum = spectrum_of(got_ref, rows_ref, wave_ref.shape[2] // 2)
    for j in range(peers):
        reads[j].wait()
        out_ref[j] = dot(wave_ref[j], spectrum).astype(bf16)


def band_kernel(
    turned, parity_ref, own_hbm, far_hbm, rest_hbm, other_hbm, toeplitz_ref, mix_ref, *rest
):
    wide_ref, x_ref, sems = rest[-3:]
    mixed_ref = rest[0]
    basis_ref = rest[1] if len(rest) > 4 else None
    kernels, group_count, width = mix_ref.shape[0], mix_ref.shape[1], mix_ref.shape[2]
    span, channels = x_ref.shape[0], x_ref.shape[2]
    per_kernel = toeplitz_ref.shape[0] // kernels
    rows = per_kernel // BLOCK
    j = pl.program_id(0)

    reach, own, wide = BAND_REACH, own_hbm.shape[0], own_hbm.shape[1]

    def fetch(moves):
        copies = []
        for source, first, count in moves:
            target = x_ref.at[pl.ds(first, count), pl.ds(0, wide), :]
            copies.append(pltpu.make_async_copy(source, target, sems.at[len(copies)]))
            copies[-1].start()
        for copy in copies:
            copy.wait()

    @pl.when((j == 0) & (parity_ref[0] == 0))
    def _():
        fetch(
            [
                (own_hbm, reach, own),
                (other_hbm, 0, reach),
                (rest_hbm, reach + own, 1),
                (far_hbm.at[pl.ds(0, reach - 1)], reach + own + 1, reach - 1),
            ]
        )

    @pl.when((j == 0) & (parity_ref[0] == 1))
    def _():
        fetch(
            [
                (own_hbm, reach, own),
                (far_hbm.at[pl.ds(1, reach - 1)], 0, reach - 1),
                (rest_hbm, reach - 1, 1),
                (other_hbm, reach + own, reach),
            ]
        )

    @pl.when(j == 0)
    def _():
        x_ref[:, wide:, :] = jnp.zeros((span, x_ref.shape[1] - wide, channels), bf16)
        wide_ref[...] = jnp.zeros_like(wide_ref)
        for b in range(kernels):
            for g in range(group_count):
                part = mix_ref[b, g]
                if turned:
                    part = part.astype(f32).T.astype(bf16)
                at = slice(g * width, (g + 1) * width)
                wide_ref[b, at, at] = part

    for w in range(WINDOWS):
        start = pl.multiple_of((j * WINDOWS + w) * BLOCK, BLOCK)
        at = pl.ds(w * BLOCK, BLOCK)
        window = x_ref[:, pl.ds(start, WINDOW), :].reshape(span * WINDOW, channels)
        basis = dot(toeplitz_ref[...], window).astype(bf16)
        total = None
        for b in range(kernels):
            part = basis[b * per_kernel : (b + 1) * per_kernel]
            if basis_ref is not None:
                basis_ref[b, :, at, :] = part.reshape(rows, BLOCK, channels)
            term = dot(part, wide_ref[b])
            total = term if total is None else total + term
        mixed_ref[:, at, :] = total.reshape(rows, BLOCK, channels)


def activation_kernel(
    valid, place_ref, spec_ref, mixed_ref, state_ref, cot_ref, next_ref, grad_ref, packed_ref, begin_ref
):
    scale = math.sqrt(2.0 / math.pi)
    step, steps = pl.program_id(0), pl.num_programs(0)
    lat_rows = state_ref.shape[0]
    peers = packed_ref.shape[0]
    for first in range(0, state_ref.shape[1], CHUNK):
        rows = pl.ds(first, CHUNK)
        for a, v, at, av in quads():
            spectra = swap_pair(
                spec_ref[2 * v, rows, at].astype(f32),
                spec_ref[2 * v + 1, rows, at].astype(f32),
            )
            grads = []
            for h in range(2):
                t = 2 * a + h
                value = spectra[h] + mixed_ref[t, rows, av]
                square = value * value
                turn = jnp.tanh(scale * value * (1.0 + 0.044715 * square))
                share = 0.5 + 0.5 * turn
                next_ref[t, rows, av] = (state_ref[t, rows, av].astype(f32) + value * share).astype(bf16)
                slope = share + (0.5 * scale) * value * (1.0 - turn * turn) * (
                    1.0 + (3.0 * 0.044715) * square
                )
                grad = cot_ref[t, rows, av].astype(f32) * slope
                grad_ref[t, rows, av] = grad.astype(bf16)
                grads.append(grad)
            low, high = swap_pair(*grads)
            packed_ref[2 * v, rows, at] = low.astype(bf16)
            packed_ref[2 * v + 1, rows, at] = high.astype(bf16)

    def edge(first, skip):
        rows = pl.ds(first, 16)
        return edge_rows(
            [grad_ref[t, rows, :].astype(f32)[skip : skip + BAND_REACH] for t in range(lat_rows)]
        )

    @pl.when(step == 0)
    def _():
        begin_ref[...] = edge(0, 0)

    @pl.when(step == steps - 1)
    def _():
        end = edge((valid - 1) // 16 * 16, (valid - 1) % 16 + 1 - BAND_REACH)
        for p in range(peers):
            to_right = p == lax.rem(place_ref[0] + 1, peers)
            packed_ref[p, valid : valid + EDGE, :] = jnp.where(to_right, end, begin_ref[...]).astype(bf16)


def finish_kernel(spec_ref, back_ref, cot_ref, out_ref):
    for first in range(0, cot_ref.shape[1], CHUNK):
        rows = pl.ds(first, CHUNK)
        for a, v, at, av in quads():
            spectra = swap_pair(
                spec_ref[2 * v, rows, at].astype(f32),
                spec_ref[2 * v + 1, rows, at].astype(f32),
            )
            for h in range(2):
                t = 2 * a + h
                out_ref[t, rows, av] = (
                    cot_ref[t, rows, av].astype(f32) + spectra[h] + back_ref[t, rows, av]
                ).astype(bf16)


def mixing_gradient_kernel(basis_ref, grad_ref, out_ref):
    kernels, lat_rows = basis_ref.shape[0], basis_ref.shape[1]
    sector = grad_ref.shape[1]
    for g in range(2):
        lanes = pl.ds(g * LANES, LANES)
        totals = [None] * kernels
        for i in range(lat_rows):
            turned = grad_ref[i, :, lanes].astype(f32).T.astype(bf16)
            for b in range(kernels):
                term = dot(turned, basis_ref[b, i, 0:sector, lanes])
                totals[b] = term if totals[b] is None else totals[b] + term
        for b in range(kernels):
            out_ref[g, b] = totals[b].T


def share_kernel(got_ref, mix_ref, out_ref):
    peers = got_ref.shape[0]
    gain_size = out_ref.shape[1] - mix_ref.shape[0]
    main = got_ref.shape[1] - 2 * gain_size
    total = jnp.concatenate([joined(got_ref[:, main:, :]), mix_ref[...]], axis=0)
    out_ref[...] = jnp.broadcast_to(total[None], out_ref.shape)


def collect_kernel(gain_rows, got_ref, gain_ref, mix_ref):
    peers, mix_rows = got_ref.shape[0], mix_ref.shape[0]
    size, mix_size = chunk_size(gain_rows, peers), chunk_size(mix_rows, peers)
    gain_ref[...] = got_ref[0 : gain_rows // size, 0:size, :].reshape(gain_rows, LANES)
    mix_ref[...] = got_ref[0 : mix_rows // mix_size, size:, :].reshape(mix_rows, LANES)


def totals_kernel(
    mix_scale, gain_scale, place_ref, gain_mine_ref, gain_other_ref, mine_ref, other_ref, mix_ref, gain_ref
):
    half = gain_ref.shape[0] // 2
    gain = (gain_mine_ref[...] + gain_other_ref[...]) * gain_scale
    gain_ref[0:half, :] = gain[:, 0:HALF]
    gain_ref[half:, :] = pltpu.roll(gain, HALF, 1)[:, 0:HALF]
    kernels, group_count, width = mix_ref.shape[0], mix_ref.shape[1], mix_ref.shape[2]
    for b in range(kernels):
        rows = slice(b * width, (b + 1) * width)
        mine, other = mine_ref[rows, :], other_ref[rows, :]
        for g in range(group_count):
            mix_ref[b, g] = jnp.where(place_ref[0] == g, mine, other) * mix_scale


def wave_kernel(column_ref, row_ref, cos_ref, sin_ref, by_wave_ref, by_point_ref):
    sectors, waves, sector = by_wave_ref.shape[0], cos_ref.shape[0], by_wave_ref.shape[2]
    c, s = cos_ref[...], sin_ref[...]
    for turned in range(2):
        orders = row_ref[...] if turned else column_ref[...]
        if turned:
            c, s = c.T, s.T
        for part in range(sectors):
            turns = jnp.broadcast_to((orders * part) & 3, c.shape)
            swap = (turns & 1) == 1
            flip_c = jnp.where((turns == 1) | (turns == 2), -1.0, 1.0)
            flip_s = jnp.where(turns <= 1, -1.0, 1.0)
            cos_part = (jnp.where(swap, s, c) * flip_c).astype(bf16)
            sin_part = (jnp.where(swap, c, s) * flip_s).astype(bf16)
            if turned:
                by_point_ref[part, :, 0:waves] = cos_part[0:sector]
                by_point_ref[part, :, waves : 2 * waves] = sin_part[0:sector]
            else:
                by_wave_ref[part, 0:waves, :] = cos_part[:, 0:sector]
                by_wave_ref[part, waves : 2 * waves, :] = sin_part[:, 0:sector]


def wave_tables(owner_order, sector, sectors):
    waves = owner_order.shape[0]
    n = jnp.arange(-(-sector // LANES) * LANES, dtype=jnp.int32)
    phases = owner_order[:, None] * n[None, :] % LONGITUDES
    angles = phases.astype(f32) * (2.0 * math.pi / LONGITUDES)
    factor = 1.0 / math.sqrt(LONGITUDES)
    c, s = jnp.cos(angles) * factor, jnp.sin(angles) * factor
    outs = [
        jax.ShapeDtypeStruct((sectors, 2 * waves, sector), bf16),
        jax.ShapeDtypeStruct((sectors, sector, 2 * waves), bf16),
    ]
    return call(wave_kernel, outs, (owner_order[:, None], owner_order[None, :], c, s), 30 * c.size)


def legendre_kernel(leg_ref, out_ref, turned_ref):
    owned, total = leg_ref.shape[0], leg_ref.shape[2]
    peers = total // 4
    t = lax.broadcasted_iota(jnp.int32, (total, total), 0)
    u = lax.broadcasted_iota(jnp.int32, (total, total), 1)
    order = (u == (t & 3) * peers + (t >> 2)).astype(f32).astype(bf16)
    order_turned = (t == (u & 3) * peers + (u >> 2)).astype(f32).astype(bf16)
    for k in range(owned):
        out_ref[k] = dot(leg_ref[k], order).astype(bf16)
        turned_ref[k] = lax.dot_general(
            order_turned, leg_ref[k], (((1,), (1,)), ((), ())), preferred_element_type=f32
        ).astype(bf16)


def toeplitz_kernel(table_ref, out_ref):
    outputs, entries = table_ref.shape[1], table_ref.shape[2]
    taps = 2 * BAND_REACH + 1
    shape = out_ref.shape[1:]
    entry = lax.broadcasted_iota(jnp.int32, (entries, shape[1]), 0)
    lane = lax.broadcasted_iota(jnp.int32, (1, shape[1]), 1)
    row_in = jnp.zeros_like(lane)
    for r in range(1, shape[1] // WINDOW):
        row_in += (lane >= r * WINDOW).astype(jnp.int32)
    n = lax.broadcasted_iota(jnp.int32, shape, 0) & (BLOCK - 1)
    tap = (lane - row_in * WINDOW) - n
    for which in range(2):
        tall = jnp.concatenate(
            [jnp.broadcast_to(table_ref[which, q : q + 1, :], (BLOCK, entries)) for q in range(outputs)],
            axis=0,
        ).astype(bf16)
        total = jnp.zeros(shape, f32)
        for d in range(taps):
            pick = (entry == taps * row_in + d).astype(f32).astype(bf16)
            total = jnp.where(tap == d, dot(tall, pick), total)
        out_ref[which] = total.astype(bf16)


def band_table(kernels_pad, offsets_pad, first_in, count_in, first_out, output_count):
    rows_kern = lax.dynamic_slice_in_dim(kernels_pad, first_in + BAND_REACH, count_in, 1)
    rows_start = lax.dynamic_slice_in_dim(offsets_pad, first_in + BAND_REACH, count_in, 0)
    targets = first_out + jnp.arange(output_count, dtype=jnp.int32)
    support_index = jnp.arange(SUPPORT, dtype=jnp.int32)
    matches = (
        rows_start[:, None, None] + support_index[None, :, None] == targets[None, None, :]
    ).astype(f32)
    return jnp.einsum("bikd,ikr->ibrd", rows_kern.astype(f32), matches, precision=highest)


def band_matrices(kernels, offsets, lat_first, lat_rows, lat_total):
    extent = lat_rows + 2 * BAND_REACH
    kernels_pad = jnp.pad(kernels, ((0, 0), (BAND_REACH, BAND_REACH), (0, 0), (0, 0)))
    offsets_pad = jnp.pad(offsets, BAND_REACH, constant_values=far_below)
    forward = band_table(
        kernels_pad, offsets_pad, lat_first, lat_rows, lat_first - BAND_REACH, extent
    )
    rows_global = lat_first - BAND_REACH + jnp.arange(extent, dtype=jnp.int32)
    inside = (rows_global >= 0) & (rows_global < lat_total)
    forward = jnp.where(inside[None, None, :, None], forward, 0.0)
    backward = band_table(
        kernels_pad, offsets_pad, lat_first - BAND_REACH, extent, lat_first, lat_rows
    )
    outputs, entries = kernels.shape[0] * lat_rows, extent * (2 * BAND_REACH + 1)
    tables = jnp.stack(
        [
            jnp.transpose(forward, (1, 0, 2, 3)).reshape(outputs, entries),
            jnp.transpose(backward[..., ::-1], (1, 2, 0, 3)).reshape(outputs, entries),
        ]
    )
    shape = jax.ShapeDtypeStruct((2, outputs * BLOCK, extent * WINDOW), bf16)
    return call(toeplitz_kernel, [shape], (tables,), 28 * math.prod(shape.shape))[0]


def exchange(x, axis):
    return lax.all_to_all(x, axis, split_axis=0, concat_axis=0, tiled=True)


def with_columns(x, circle):
    peers = lax.axis_size("lon")
    me = lax.axis_index("lon")
    lat_rows, sector, channels = x.shape
    edges = circle[:, sector:].reshape(peers, lat_rows, EDGE // lat_rows, channels)[:, :, :BAND_REACH]
    before = lax.dynamic_index_in_dim(edges, lax.rem(me + peers - 1, peers), 0, False)
    after = lax.dynamic_index_in_dim(edges, lax.rem(me + 1, peers), 0, False)
    spare = jnp.zeros((lat_rows, -(sector + 2 * BAND_REACH) % 16, channels), bf16)
    return jnp.concatenate([before, x, after, spare], axis=1)


def pairs():
    return [(i, i ^ 1) for i in range(lax.axis_size("lat"))]


def swapped_rows(x, even):
    return lax.ppermute(jnp.where(even, x[:BAND_REACH], x[1 : BAND_REACH + 1]), "lat", pairs())


def relayed_rows(far):
    peers = lax.axis_size("lat")
    relay = [(i, (i + 2) % peers if i % 2 == 0 else (i - 2) % peers) for i in range(peers)]
    return lax.ppermute(far, "lat", relay)


def rest_rows(x, even):
    return lax.ppermute(jnp.where(even, x[BAND_REACH:], x[:1]), "lat", pairs())


def on_device(states, cotangent, kernels, offsets, mixing, legendre, owner_order, spectral_gain):
    fields = states[0]
    cot = cotangent[0]
    lat_rows, sector, channels = fields.shape
    lon_index = lax.axis_index("lon")
    lat_index = lax.axis_index("lat")
    ens_index = lax.axis_index("ens")
    lon_count = lax.axis_size("lon")
    lat_count = lax.axis_size("lat")
    members = states.shape[0] * lax.axis_size("ens")
    lat_first = lat_index * lat_rows
    lat_total = lat_rows * lat_count
    kernel_number, group_count, width = mixing.shape[0], mixing.shape[1], mixing.shape[2]
    quarter = channels // lon_count
    owned, degrees = legendre.shape[0], legendre.shape[1]
    waves = owner_order.shape[0]
    main = 4 * owned
    gain_size = chunk_size(degrees // 2, lat_count)
    mix_size = chunk_size(kernel_number * width, lat_count)
    even = lat_index % 2 == 0
    blocks = WINDOWS * -(-sector // (WINDOWS * BLOCK))
    padded = blocks * BLOCK
    padded_in = padded + WINDOW - BLOCK
    sds = jax.ShapeDtypeStruct
    field_shape = sds((lat_rows, sector, channels), bf16)
    wide_shape = sds((lat_rows, padded, channels), f32)

    by_wave, by_point = wave_tables(owner_order, sector, lon_count)
    orders = lax.dynamic_slice_in_dim(owner_order, lat_index * owned, owned, 0)
    gains = lax.dynamic_slice_in_dim(spectral_gain, lon_index * quarter, quarter, 1).astype(f32)
    gains = jnp.concatenate([gains, gains], axis=1)
    leg, leg_turned = call(
        legendre_kernel,
        [sds(legendre.shape, bf16), sds((owned, lat_total, degrees), bf16)],
        (legendre,),
        4 * legendre.size * lat_total,
    )
    matrices = band_matrices(kernels, offsets, lat_first, lat_rows, lat_total)
    place = jnp.reshape(lon_index, (1,))
    parity = jnp.reshape(lat_index % 2, (1,))
    extent = lat_rows + 2 * BAND_REACH

    transform_flops = 4 * waves * LONGITUDES * lat_rows * quarter
    legendre_flops = 4 * owned * degrees * lat_total * 2 * quarter
    band_flops = 2 * blocks * matrices[0].size * channels
    row_scratch = pltpu.VMEM((4 * waves, LANES), f32)
    leg_scratch = [
        pltpu.VMEM((owned, degrees, LANES), f32),
        pltpu.VMEM(leg.shape, bf16),
        pltpu.VMEM(leg_turned.shape, bf16),
        pltpu.SemaphoreType.DMA((3, PARTS)),
    ]
    sent_shape = pltpu.HBM((lon_count, sector + EDGE, channels), bf16)
    spectrum_shape = pltpu.HBM((lon_count, sector, channels), bf16)
    tile = pl.BlockSpec((lat_rows, TILE, channels), lambda j: (0, j, 0))
    tiles = pl.cdiv(sector, TILE)

    def whole(x):
        return pl.BlockSpec(x.shape, lambda j: (0,) * x.ndim)

    def synthesized(got):
        return call(
            synthesis_kernel,
            [spectrum_shape],
            (got, by_point),
            transform_flops,
            [row_scratch, pltpu.VMEM(by_point.shape, bf16), pltpu.SemaphoreType.DMA((lon_count,))],
            places={1: pl.ANY},
        )[0]

    def band(x, far, other, which, turned):
        rest = rest_rows(x, even)
        matrix = matrices[which]
        outs = [pltpu.HBM(wide_shape.shape, f32)]
        specs = [pl.BlockSpec((lat_rows, WINDOWS * BLOCK, channels), lambda j: (0, j, 0))]
        if not turned:
            outs.append(pltpu.HBM((kernel_number, lat_rows, padded, channels), bf16))
            specs.append(
                pl.BlockSpec((kernel_number, lat_rows, WINDOWS * BLOCK, channels), lambda j: (0, 0, j, 0))
            )
        return call(
            functools.partial(band_kernel, turned),
            outs,
            (parity, hbm(x), hbm(far), hbm(rest), hbm(other), matrix, mixing),
            band_flops * 12,
            [
                pltpu.VMEM((kernel_number, channels, channels), bf16),
                pltpu.VMEM((extent, padded_in, channels), bf16),
                pltpu.SemaphoreType.DMA((4,)),
            ],
            grid=(blocks // WINDOWS,),
            blocks=[pl.BlockSpec(memory_space=SMEM)]
            + [pl.BlockSpec(memory_space=pl.ANY)] * 4
            + [whole(matrix), whole(mixing)],
            outs=specs,
        )

    (packed,) = call(pack_kernel, [sent_shape], (place, fields), 0, places={0: SMEM})
    circle = exchange(packed, "lon")
    circle, by_wave, by_point, leg, leg_turned, matrices, gains = lax.optimization_barrier(
        (circle, by_wave, by_point, leg, leg_turned, matrices, gains)
    )
    by_point, leg, leg_turned = hbm(by_point), hbm(leg), hbm(leg_turned)
    extended = with_columns(fields, circle)
    far = swapped_rows(extended, even)
    (analysed,) = call(
        analysis_kernel,
        [pltpu.HBM((lat_count, main, LANES), bf16)],
        (circle, by_wave),
        transform_flops,
        [row_scratch],
    )
    owned_rows = exchange(analysed, "lat")
    synthesis, coeffs = call(
        legendre_forward_kernel,
        [pltpu.HBM((lat_count, main, LANES), bf16), pltpu.HBM((owned, degrees, LANES), f32)],
        (orders, owned_rows, leg, leg_turned, gains),
        legendre_flops,
        [row_scratch, row_scratch] + leg_scratch,
        places={0: SMEM, 2: pl.ANY, 3: pl.ANY, -2: pl.ANY},
    )
    returned = exchange(synthesis, "lat")
    other = relayed_rows(far)
    spectrum = exchange(synthesized(returned), "lon")
    mixed, basis = band(extended, far, other, 0, False)
    next_state, grad_pre, packed_back = call(
        functools.partial(activation_kernel, sector - (tiles - 1) * TILE),
        [field_shape, pltpu.HBM(field_shape.shape, bf16), sent_shape],
        (place, hbm(spectrum), hbm(mixed), hbm(fields), hbm(cot)),
        40 * fields.size,
        [pltpu.VMEM((EDGE, channels), f32)],
        grid=(tiles,),
        blocks=[pl.BlockSpec(memory_space=SMEM), tile, tile, tile, tile],
        outs=[tile, tile, tile],
    )

    circle_back = exchange(packed_back, "lon")
    (mix_part,) = call(
        mixing_gradient_kernel,
        [sds((group_count, kernel_number, width, width), f32)],
        (basis, grad_pre),
        2 * kernel_number * fields.size * width,
    )
    mix_part = mix_part.reshape(group_count, kernel_number * width, width)
    swap = [(0, 1), (1, 0)]
    kept = lax.dynamic_index_in_dim(mix_part, ens_index, 0, False)
    sent = lax.dynamic_index_in_dim(mix_part, 1 - ens_index, 0, False)
    mix_got = lax.ppermute(sent, "ens", swap)
    circle_back, kept, mix_got = lax.optimization_barrier((circle_back, kept, mix_got))
    extended_back = with_columns(grad_pre, circle_back)
    far_back = swapped_rows(extended_back, even)
    (analysed_back,) = call(
        analysis_kernel,
        [pltpu.HBM((lat_count, main + 2 * mix_size, LANES), bf16)],
        (circle_back, by_wave, hbm(kept), hbm(mix_got)),
        transform_flops,
        [row_scratch, pltpu.VMEM((2,) + kept.shape, f32), pltpu.SemaphoreType.DMA((2,))],
        places={2: pl.ANY, 3: pl.ANY},
    )
    owned_back = exchange(analysed_back, "lat")
    synthesis_back, mix_sum = call(
        legendre_backward_kernel,
        [pltpu.HBM((lat_count, main + 2 * gain_size, LANES), bf16), sds((mix_size, LANES), f32)],
        (orders, owned_back, leg, leg_turned, gains, hbm(coeffs)),
        legendre_flops,
        [row_scratch, row_scratch, pltpu.VMEM((degrees, LANES), f32)] + leg_scratch,
        places={0: SMEM, 2: pl.ANY, 3: pl.ANY, 5: pl.ANY},
    )
    returned_back = exchange(synthesis_back, "lat")
    other_back = relayed_rows(far_back)
    for bit in (1, 2):
        mix_sum += lax.ppermute(mix_sum, "lon", [(i, i ^ bit) for i in range(lon_count)])
    returned_back, other_back, mix_sum = lax.optimization_barrier((returned_back, other_back, mix_sum))
    shares = call(
        share_kernel,
        [sds((lat_count, gain_size + mix_size, LANES), f32)],
        (returned_back, mix_sum),
        0,
    )[0]
    shares = exchange(shares, "lat")
    spectrum_back = exchange(synthesized(returned_back), "lon")
    (backward,) = band(extended_back, far_back, other_back, 1, True)
    (grad_state,) = call(
        finish_kernel,
        [field_shape],
        (hbm(spectrum_back), hbm(backward), hbm(cot)),
        4 * fields.size,
        grid=(tiles,),
        blocks=[tile, tile, tile],
        outs=[tile],
    )

    mix_scale = 1.0 / math.sqrt(members * lat_total * LONGITUDES)
    gain_scale = 1.0 / math.sqrt(2 * members * degrees)
    gain_mine, mix_mine = call(
        functools.partial(collect_kernel, degrees // 2),
        [sds((degrees // 2, LANES), f32), sds((kernel_number * width, LANES), f32)],
        (shares,),
        0,
    )
    mix_other = lax.ppermute(mix_mine, "ens", swap)
    gain_other = lax.ppermute(gain_mine, "ens", swap)
    grad_mixing, grad_gain = call(
        functools.partial(totals_kernel, mix_scale, gain_scale),
        [sds(mixing.shape, f32), sds((degrees, quarter), f32)],
        (jnp.reshape(ens_index, (1,)), gain_mine, gain_other, mix_mine, mix_other),
        0,
        places={0: SMEM},
    )
    return (next_state[None], grad_state[None], grad_mixing, grad_gain)


def solution(mesh):
    in_specs = (
        P("ens", "lat", "lon", None),
        P("ens", "lat", "lon", None),
        P(),
        P(),
        P(),
        P("lat", None, None),
        P(),
        P(),
    )
    out_specs = (P("ens", "lat", "lon", None), P("ens", "lat", "lon", None), P(), P(None, "lon"))
    return jax.shard_map(
        on_device, mesh=mesh, in_specs=in_specs, out_specs=out_specs, check_vma=False
    )
```

```python
import functools
import math

import jax
import jax.numpy as jnp
from jax import lax
from jax.experimental import pallas as pl
from jax.experimental.pallas import tpu as pltpu
from jax.sharding import PartitionSpec as P

LONGITUDES = 1440
BAND_REACH = 3
SUPPORT = 4
HALF = 64
LANES = 128
BLOCK = 32
WINDOW = 48
CHUNK = 48
TILE = 96
WINDOWS = 3
EDGE = 16
PARTS = 3

bf16 = jnp.bfloat16
f32 = jnp.float32
highest = lax.Precision.HIGHEST
far_below = -1000000


VMEM = pltpu.VMEM
SMEM = pltpu.SMEM


def call(kernel, out_shape, args, flops, scratch=(), places=None, grid=(), blocks=None, outs=None, limit=24):
    moved = sum(a.size * a.dtype.itemsize for a in args)
    moved += sum(math.prod(o.shape) * jnp.dtype(o.dtype).itemsize for o in out_shape)
    places = places or {}
    specs = blocks or [pl.BlockSpec(memory_space=places.get(i, VMEM)) for i in range(len(args))]
    out_specs = outs or [
        pl.BlockSpec(memory_space=places[-1 - i]) if -1 - i in places else pl.BlockSpec()
        for i in range(len(out_shape))
    ]
    return pl.pallas_call(
        kernel,
        grid=grid,
        out_shape=out_shape,
        in_specs=specs,
        out_specs=out_specs,
        scratch_shapes=list(scratch),
        compiler_params=pltpu.CompilerParams(vmem_limit_bytes=limit * 1024 * 1024),
        cost_estimate=pl.CostEstimate(
            flops=int(flops), bytes_accessed=int(moved), transcendentals=0
        ),
    )(*args)


def hbm(x):
    return pltpu.with_memory_space_constraint(x, pltpu.HBM)


def dot(a, b):
    return lax.dot_general(a, b, (((1,), (0,)), ((), ())), preferred_element_type=f32)


def swap_pair(first, second):
    left = lax.broadcasted_iota(jnp.int32, first.shape, 1) < HALF
    low = jnp.where(left, first, pltpu.roll(second, HALF, 1))
    high = jnp.where(left, pltpu.roll(first, HALF, 1), second)
    return low, high


def quads():
    for a in range(2):
        for v in range(2):
            yield a, v, pl.ds(a * LANES, LANES), pl.ds(v * LANES, LANES)


def edge_rows(columns):
    rows = []
    for column in columns:
        rows += [column, jnp.zeros((1, column.shape[1]), f32)]
    return jnp.concatenate(rows, axis=0)


def pack_kernel(place_ref, x_ref, out_ref):
    sector = x_ref.shape[1]
    for first in range(0, sector, CHUNK):
        rows = pl.ds(first, min(CHUNK, sector - first))
        for a, v, at, av in quads():
            low, high = swap_pair(
                x_ref[2 * a, rows, av].astype(f32), x_ref[2 * a + 1, rows, av].astype(f32)
            )
            out_ref[2 * v, rows, at] = low.astype(bf16)
            out_ref[2 * v + 1, rows, at] = high.astype(bf16)
    lat_rows = x_ref.shape[0]
    begin = edge_rows([x_ref[t, 0:16, :].astype(f32)[:BAND_REACH] for t in range(lat_rows)])
    end = edge_rows([x_ref[t, sector - 8 : sector, :].astype(f32)[8 - BAND_REACH :] for t in range(lat_rows)])
    peers = out_ref.shape[0]
    for p in range(peers):
        to_right = p == lax.rem(place_ref[0] + 1, peers)
        out_ref[p, sector : sector + EDGE, :] = jnp.where(to_right, end, begin).astype(bf16)


def analysis_kernel(circle_ref, wave_ref, *rest):
    out_ref, rows_ref = rest[2:4] if len(rest) > 2 else rest
    copies = []
    if len(rest) > 2:
        terms_ref, sems = rest[4:]
        for j in range(2):
            copies.append(pltpu.make_async_copy(rest[j], terms_ref.at[j], sems.at[j]))
            copies[j].start()
    waves, sector = wave_ref.shape[1] // 2, wave_ref.shape[2]
    sums = []
    for r in range(2):
        total = None
        for s in range(wave_ref.shape[0]):
            term = dot(wave_ref[s, r * waves : (r + 1) * waves, :], circle_ref[s, 0:sector, :])
            total = term if total is None else total + term
        sums.append(total)
    for a in range(2):
        lanes = slice(a * LANES, (a + 1) * LANES)
        low, high = swap_pair(sums[0][:, lanes], sums[1][:, lanes])
        rows_ref[pl.ds(2 * a, waves, stride=4), :] = low
        rows_ref[pl.ds(2 * a + 1, waves, stride=4), :] = high
    peers = out_ref.shape[0]
    main = 4 * waves // peers
    out_ref[:, 0:main, :] = rows_ref[...].reshape(peers, main, LANES).astype(bf16)
    if copies:
        for copy in copies:
            copy.wait()
        out_ref[:, main:, :] = split_chunks(terms_ref[0] + terms_ref[1], peers)[:, 0 : out_ref.shape[1] - main, :]


def chunk_size(rows, peers):
    return 8 * -(-rows // (8 * peers))


def split_chunks(total, peers):
    high = total.astype(bf16).astype(f32)
    low = total - high
    size = chunk_size(total.shape[0], peers)
    used = total.shape[0] // size
    both = jnp.concatenate(
        [high.reshape(used, size, LANES), low.reshape(used, size, LANES)], axis=1
    )
    if used < peers:
        both = jnp.concatenate([both, jnp.zeros((peers - used, 2 * size, LANES), f32)], axis=0)
    return both.astype(bf16)


def joined(got):
    total = jnp.sum(got.astype(f32), axis=0)
    size = total.shape[0] // 2
    return total[:size] + total[size:]


def legendre_steps(order_ref, rows_in_ref, leg_ref, leg_turned_ref, gain_ref, rows_out_ref, peers, part, use):
    owned, degrees = leg_ref.shape[0], leg_ref.shape[1]
    step = 4 * owned
    degree = lax.broadcasted_iota(jnp.int32, (degrees, LANES), 0)
    for k in part:
        field = jnp.concatenate(
            [rows_in_ref[pl.ds(4 * k + t, peers, stride=step), :] for t in range(4)], axis=0
        ).astype(bf16)
        coeffs = dot(leg_ref[k], field)
        coeffs = jnp.where(degree >= order_ref[k], coeffs, 0.0)
        use(k, coeffs)
        weighted = (coeffs * gain_ref[...]).astype(bf16)
        synthesis = dot(leg_turned_ref[k], weighted)
        for t in range(4):
            rows_out_ref[pl.ds(4 * k + t, peers, stride=step), :] = synthesis[
                t * peers : (t + 1) * peers
            ]


def parts(owned):
    count = owned // PARTS
    return [(p, pl.ds(p * count, count), range(p * count, (p + 1) * count)) for p in range(PARTS)]


def legendre_forward_kernel(
    order_ref,
    got_ref,
    leg_hbm,
    leg_turned_hbm,
    gain_ref,
    out_ref,
    coeffs_hbm,
    rows_in_ref,
    rows_out_ref,
    held_ref,
    leg_ref,
    leg_turned_ref,
    sems,
):
    peers = got_ref.shape[0]
    main = rows_in_ref.shape[0] // peers
    reads, writes = [], []
    for p, at, _ in parts(leg_ref.shape[0]):
        reads.append(
            [
                pltpu.make_async_copy(leg_hbm.at[at], leg_ref.at[at], sems.at[0, p]),
                pltpu.make_async_copy(leg_turned_hbm.at[at], leg_turned_ref.at[at], sems.at[1, p]),
            ]
        )
        for copy in reads[p]:
            copy.start()
    rows_in_ref[...] = got_ref[...].astype(f32).reshape(peers * main, LANES)

    def use(k, coeffs):
        held_ref[k] = coeffs

    for p, at, part in parts(leg_ref.shape[0]):
        for copy in reads[p]:
            copy.wait()
        legendre_steps(
            order_ref, rows_in_ref, leg_ref, leg_turned_ref, gain_ref, rows_out_ref, peers, part, use
        )
        writes.append(pltpu.make_async_copy(held_ref.at[at], coeffs_hbm.at[at], sems.at[2, p]))
        writes[p].start()
    out_ref[...] = rows_out_ref[...].reshape(peers, main, LANES).astype(bf16)
    for copy in writes:
        copy.wait()


def legendre_backward_kernel(
    order_ref,
    got_ref,
    leg_hbm,
    leg_turned_hbm,
    gain_ref,
    coeffs_hbm,
    out_ref,
    mix_ref,
    rows_in_ref,
    rows_out_ref,
    sum_ref,
    held_ref,
    leg_ref,
    leg_turned_ref,
    sems,
):
    peers = got_ref.shape[0]
    main = rows_in_ref.shape[0] // peers
    reads = []
    for p, at, _ in parts(leg_ref.shape[0]):
        reads.append(
            [
                pltpu.make_async_copy(leg_hbm.at[at], leg_ref.at[at], sems.at[0, p]),
                pltpu.make_async_copy(leg_turned_hbm.at[at], leg_turned_ref.at[at], sems.at[1, p]),
                pltpu.make_async_copy(coeffs_hbm.at[at], held_ref.at[at], sems.at[2, p]),
            ]
        )
        for copy in reads[p]:
            copy.start()
    rows_in_ref[...] = got_ref[:, 0:main, :].astype(f32).reshape(peers * main, LANES)
    mix_ref[...] = jnp.sum(got_ref[:, main:, :].astype(f32), axis=0)

    def use(k, coeffs):
        term = coeffs * held_ref[k]
        if k == 0:
            sum_ref[...] = term
        else:
            sum_ref[...] += term

    for p, _, part in parts(leg_ref.shape[0]):
        for copy in reads[p]:
            copy.wait()
        legendre_steps(
            order_ref, rows_in_ref, leg_ref, leg_turned_ref, gain_ref, rows_out_ref, peers, part, use
        )
    out_ref[:, 0:main, :] = rows_out_ref[...].reshape(peers, main, LANES).astype(bf16)
    total = sum_ref[...]
    total = total + pltpu.roll(total, HALF, 1)
    half = total.shape[0] // 2
    left = lax.broadcasted_iota(jnp.int32, (half, LANES), 1) < HALF
    out_ref[:, main:, :] = split_chunks(jnp.where(left, total[:half], total[half:]), peers)


def spectrum_of(got_ref, rows_ref, waves):
    peers = got_ref.shape[0]
    main = 4 * waves // peers
    rows_ref[...] = got_ref[:, 0:main, :].astype(f32).reshape(4 * waves, LANES)
    low, high = [], []
    for a in range(2):
        lo, hi = swap_pair(
            rows_ref[pl.ds(2 * a, waves, stride=4), :], rows_ref[pl.ds(2 * a + 1, waves, stride=4), :]
        )
        low.append(lo)
        high.append(hi)
    return jnp.concatenate(
        [jnp.concatenate(low, axis=1), jnp.concatenate(high, axis=1)], axis=0
    ).astype(bf16)


def synthesis_kernel(got_ref, wave_hbm, out_ref, rows_ref, wave_ref, sems):
    peers = out_ref.shape[0]
    reads = []
    for j in range(peers):
        reads.append(pltpu.make_async_copy(wave_hbm.at[j], wave_ref.at[j], sems.at[j]))
        reads[j].start()
    spectrum = spectrum_of(got_ref, rows_ref, wave_ref.shape[2] // 2)
    for j in range(peers):
        reads[j].wait()
        out_ref[j] = dot(wave_ref[j], spectrum).astype(bf16)


def band_kernel(
    turned, parity_ref, own_hbm, far_hbm, rest_hbm, other_hbm, toeplitz_ref, mix_ref, *rest
):
    wide_ref, x_ref, sems = rest[-3:]
    mixed_ref = rest[0]
    basis_ref = rest[1] if len(rest) > 4 else None
    kernels, group_count, width = mix_ref.shape[0], mix_ref.shape[1], mix_ref.shape[2]
    span, channels = x_ref.shape[0], x_ref.shape[2]
    per_kernel = toeplitz_ref.shape[0] // kernels
    rows = per_kernel // BLOCK
    j = pl.program_id(0)

    reach, own, wide = BAND_REACH, own_hbm.shape[0], own_hbm.shape[1]

    def fetch(moves):
        copies = []
        for source, first, count in moves:
            target = x_ref.at[pl.ds(first, count), pl.ds(0, wide), :]
            copies.append(pltpu.make_async_copy(source, target, sems.at[len(copies)]))
            copies[-1].start()
        for copy in copies:
            copy.wait()

    @pl.when((j == 0) & (parity_ref[0] == 0))
    def _():
        fetch(
            [
                (own_hbm, reach, own),
                (other_hbm, 0, reach),
                (rest_hbm, reach + own, 1),
                (far_hbm.at[pl.ds(0, reach - 1)], reach + own + 1, reach - 1),
            ]
        )

    @pl.when((j == 0) & (parity_ref[0] == 1))
    def _():
        fetch(
            [
                (own_hbm, reach, own),
                (far_hbm.at[pl.ds(1, reach - 1)], 0, reach - 1),
                (rest_hbm, reach - 1, 1),
                (other_hbm, reach + own, reach),
            ]
        )

    @pl.when(j == 0)
    def _():
        x_ref[:, wide:, :] = jnp.zeros((span, x_ref.shape[1] - wide, channels), bf16)
        wide_ref[...] = jnp.zeros_like(wide_ref)
        for b in range(kernels):
            for g in range(group_count):
                part = mix_ref[b, g]
                if turned:
                    part = part.astype(f32).T.astype(bf16)
                at = slice(g * width, (g + 1) * width)
                wide_ref[b, at, at] = part

    for w in range(WINDOWS):
        start = pl.multiple_of((j * WINDOWS + w) * BLOCK, BLOCK)
        at = pl.ds(w * BLOCK, BLOCK)
        window = x_ref[:, pl.ds(start, WINDOW), :].reshape(span * WINDOW, channels)
        basis = dot(toeplitz_ref[...], window).astype(bf16)
        total = None
        for b in range(kernels):
            part = basis[b * per_kernel : (b + 1) * per_kernel]
            if basis_ref is not None:
                basis_ref[b, :, at, :] = part.reshape(rows, BLOCK, channels)
            term = dot(part, wide_ref[b])
            total = term if total is None else total + term
        mixed_ref[:, at, :] = total.reshape(rows, BLOCK, channels)


def activation_kernel(
    valid, place_ref, spec_ref, mixed_ref, state_ref, cot_ref, next_ref, grad_ref, packed_ref, begin_ref
):
    scale = math.sqrt(2.0 / math.pi)
    step, steps = pl.program_id(0), pl.num_programs(0)
    lat_rows = state_ref.shape[0]
    peers = packed_ref.shape[0]
    for first in range(0, state_ref.shape[1], CHUNK):
        rows = pl.ds(first, CHUNK)
        for a, v, at, av in quads():
            spectra = swap_pair(
                spec_ref[2 * v, rows, at].astype(f32),
                spec_ref[2 * v + 1, rows, at].astype(f32),
            )
            grads = []
            for h in range(2):
                t = 2 * a + h
                value = spectra[h] + mixed_ref[t, rows, av]
                square = value * value
                turn = jnp.tanh(scale * value * (1.0 + 0.044715 * square))
                share = 0.5 + 0.5 * turn
                next_ref[t, rows, av] = (state_ref[t, rows, av].astype(f32) + value * share).astype(bf16)
                slope = share + (0.5 * scale) * value * (1.0 - turn * turn) * (
                    1.0 + (3.0 * 0.044715) * square
                )
                grad = cot_ref[t, rows, av].astype(f32) * slope
                grad_ref[t, rows, av] = grad.astype(bf16)
                grads.append(grad)
            low, high = swap_pair(*grads)
            packed_ref[2 * v, rows, at] = low.astype(bf16)
            packed_ref[2 * v + 1, rows, at] = high.astype(bf16)

    def edge(first, skip):
        rows = pl.ds(first, 16)
        return edge_rows(
            [grad_ref[t, rows, :].astype(f32)[skip : skip + BAND_REACH] for t in range(lat_rows)]
        )

    @pl.when(step == 0)
    def _():
        begin_ref[...] = edge(0, 0)

    @pl.when(step == steps - 1)
    def _():
        end = edge((valid - 1) // 16 * 16, (valid - 1) % 16 + 1 - BAND_REACH)
        for p in range(peers):
            to_right = p == lax.rem(place_ref[0] + 1, peers)
            packed_ref[p, valid : valid + EDGE, :] = jnp.where(to_right, end, begin_ref[...]).astype(bf16)


def finish_kernel(spec_ref, back_ref, cot_ref, out_ref):
    for first in range(0, cot_ref.shape[1], CHUNK):
        rows = pl.ds(first, CHUNK)
        for a, v, at, av in quads():
            spectra = swap_pair(
                spec_ref[2 * v, rows, at].astype(f32),
                spec_ref[2 * v + 1, rows, at].astype(f32),
            )
            for h in range(2):
                t = 2 * a + h
                out_ref[t, rows, av] = (
                    cot_ref[t, rows, av].astype(f32) + spectra[h] + back_ref[t, rows, av]
                ).astype(bf16)


def mixing_gradient_kernel(basis_ref, grad_ref, out_ref):
    kernels, lat_rows = basis_ref.shape[0], basis_ref.shape[1]
    sector = grad_ref.shape[1]
    for g in range(2):
        lanes = pl.ds(g * LANES, LANES)
        totals = [None] * kernels
        for i in range(lat_rows):
            turned = grad_ref[i, :, lanes].astype(f32).T.astype(bf16)
            for b in range(kernels):
                term = dot(turned, basis_ref[b, i, 0:sector, lanes])
                totals[b] = term if totals[b] is None else totals[b] + term
        for b in range(kernels):
            out_ref[g, b] = totals[b].T


def share_kernel(got_ref, mix_ref, out_ref):
    peers = got_ref.shape[0]
    gain_size = out_ref.shape[1] // 2 - mix_ref.shape[0]
    main = got_ref.shape[1] - 2 * gain_size
    total = jnp.concatenate([joined(got_ref[:, main:, :]), mix_ref[...]], axis=0)
    high = total.astype(bf16).astype(f32)
    both = jnp.concatenate([high, total - high], axis=0).astype(bf16)
    out_ref[...] = jnp.broadcast_to(both[None], out_ref.shape)


def collect_kernel(gain_rows, got_ref, gain_ref, mix_ref):
    peers, mix_rows = got_ref.shape[0], mix_ref.shape[0]
    size, mix_size = chunk_size(gain_rows, peers), chunk_size(mix_rows, peers)
    half = got_ref.shape[1] // 2
    total = got_ref[:, 0:half, :].astype(f32) + got_ref[:, half:, :].astype(f32)
    gain_ref[...] = total[0 : gain_rows // size, 0:size, :].reshape(gain_rows, LANES)
    mix_ref[...] = total[0 : mix_rows // mix_size, size:, :].reshape(mix_rows, LANES)


def totals_kernel(
    mix_scale, gain_scale, place_ref, gain_mine_ref, gain_other_ref, mine_ref, other_ref, mix_ref, gain_ref
):
    half = gain_ref.shape[0] // 2
    gain = (gain_mine_ref[...] + gain_other_ref[...]) * gain_scale
    gain_ref[0:half, :] = gain[:, 0:HALF]
    gain_ref[half:, :] = pltpu.roll(gain, HALF, 1)[:, 0:HALF]
    kernels, group_count, width = mix_ref.shape[0], mix_ref.shape[1], mix_ref.shape[2]
    for b in range(kernels):
        rows = slice(b * width, (b + 1) * width)
        mine, other = mine_ref[rows, :], other_ref[rows, :]
        for g in range(group_count):
            mix_ref[b, g] = jnp.where(place_ref[0] == g, mine, other) * mix_scale


def wave_kernel(column_ref, row_ref, cos_ref, sin_ref, by_wave_ref, by_point_ref):
    sectors, waves, sector = by_wave_ref.shape[0], cos_ref.shape[0], by_wave_ref.shape[2]
    c, s = cos_ref[...], sin_ref[...]
    for turned in range(2):
        orders = row_ref[...] if turned else column_ref[...]
        if turned:
            c, s = c.T, s.T
        for part in range(sectors):
            turns = jnp.broadcast_to((orders * part) & 3, c.shape)
            swap = (turns & 1) == 1
            flip_c = jnp.where((turns == 1) | (turns == 2), -1.0, 1.0)
            flip_s = jnp.where(turns <= 1, -1.0, 1.0)
            cos_part = (jnp.where(swap, s, c) * flip_c).astype(bf16)
            sin_part = (jnp.where(swap, c, s) * flip_s).astype(bf16)
            if turned:
                by_point_ref[part, :, 0:waves] = cos_part[0:sector]
                by_point_ref[part, :, waves : 2 * waves] = sin_part[0:sector]
            else:
                by_wave_ref[part, 0:waves, :] = cos_part[:, 0:sector]
                by_wave_ref[part, waves : 2 * waves, :] = sin_part[:, 0:sector]


def wave_tables(owner_order, sector, sectors):
    waves = owner_order.shape[0]
    n = jnp.arange(-(-sector // LANES) * LANES, dtype=jnp.int32)
    phases = owner_order[:, None] * n[None, :] % LONGITUDES
    angles = phases.astype(f32) * (2.0 * math.pi / LONGITUDES)
    factor = 1.0 / math.sqrt(LONGITUDES)
    c, s = jnp.cos(angles) * factor, jnp.sin(angles) * factor
    outs = [
        jax.ShapeDtypeStruct((sectors, 2 * waves, sector), bf16),
        jax.ShapeDtypeStruct((sectors, sector, 2 * waves), bf16),
    ]
    return call(wave_kernel, outs, (owner_order[:, None], owner_order[None, :], c, s), 30 * c.size)


def legendre_kernel(leg_ref, out_ref, turned_ref):
    owned, total = leg_ref.shape[0], leg_ref.shape[2]
    peers = total // 4
    t = lax.broadcasted_iota(jnp.int32, (total, total), 0)
    u = lax.broadcasted_iota(jnp.int32, (total, total), 1)
    order = (u == (t & 3) * peers + (t >> 2)).astype(f32).astype(bf16)
    order_turned = (t == (u & 3) * peers + (u >> 2)).astype(f32).astype(bf16)
    for k in range(owned):
        out_ref[k] = dot(leg_ref[k], order).astype(bf16)
        turned_ref[k] = lax.dot_general(
            order_turned, leg_ref[k], (((1,), (1,)), ((), ())), preferred_element_type=f32
        ).astype(bf16)


def toeplitz_kernel(table_ref, out_ref):
    outputs, entries = table_ref.shape[1], table_ref.shape[2]
    taps = 2 * BAND_REACH + 1
    shape = out_ref.shape[1:]
    entry = lax.broadcasted_iota(jnp.int32, (entries, shape[1]), 0)
    lane = lax.broadcasted_iota(jnp.int32, (1, shape[1]), 1)
    row_in = jnp.zeros_like(lane)
    for r in range(1, shape[1] // WINDOW):
        row_in += (lane >= r * WINDOW).astype(jnp.int32)
    n = lax.broadcasted_iota(jnp.int32, shape, 0) & (BLOCK - 1)
    tap = (lane - row_in * WINDOW) - n
    for which in range(2):
        tall = jnp.concatenate(
            [jnp.broadcast_to(table_ref[which, q : q + 1, :], (BLOCK, entries)) for q in range(outputs)],
            axis=0,
        ).astype(bf16)
        total = jnp.zeros(shape, f32)
        for d in range(taps):
            pick = (entry == taps * row_in + d).astype(f32).astype(bf16)
            total = jnp.where(tap == d, dot(tall, pick), total)
        out_ref[which] = total.astype(bf16)


def band_table(kernels_pad, offsets_pad, first_in, count_in, first_out, output_count):
    rows_kern = lax.dynamic_slice_in_dim(kernels_pad, first_in + BAND_REACH, count_in, 1)
    rows_start = lax.dynamic_slice_in_dim(offsets_pad, first_in + BAND_REACH, count_in, 0)
    targets = first_out + jnp.arange(output_count, dtype=jnp.int32)
    support_index = jnp.arange(SUPPORT, dtype=jnp.int32)
    matches = (
        rows_start[:, None, None] + support_index[None, :, None] == targets[None, None, :]
    ).astype(f32)
    return jnp.einsum("bikd,ikr->ibrd", rows_kern.astype(f32), matches, precision=highest)


def band_matrices(kernels, offsets, lat_first, lat_rows, lat_total):
    extent = lat_rows + 2 * BAND_REACH
    kernels_pad = jnp.pad(kernels, ((0, 0), (BAND_REACH, BAND_REACH), (0, 0), (0, 0)))
    offsets_pad = jnp.pad(offsets, BAND_REACH, constant_values=far_below)
    forward = band_table(
        kernels_pad, offsets_pad, lat_first, lat_rows, lat_first - BAND_REACH, extent
    )
    rows_global = lat_first - BAND_REACH + jnp.arange(extent, dtype=jnp.int32)
    inside = (rows_global >= 0) & (rows_global < lat_total)
    forward = jnp.where(inside[None, None, :, None], forward, 0.0)
    backward = band_table(
        kernels_pad, offsets_pad, lat_first - BAND_REACH, extent, lat_first, lat_rows
    )
    outputs, entries = kernels.shape[0] * lat_rows, extent * (2 * BAND_REACH + 1)
    tables = jnp.stack(
        [
            jnp.transpose(forward, (1, 0, 2, 3)).reshape(outputs, entries),
            jnp.transpose(backward[..., ::-1], (1, 2, 0, 3)).reshape(outputs, entries),
        ]
    )
    shape = jax.ShapeDtypeStruct((2, outputs * BLOCK, extent * WINDOW), bf16)
    return call(toeplitz_kernel, [shape], (tables,), 28 * math.prod(shape.shape))[0]


def exchange(x, axis):
    return lax.all_to_all(x, axis, split_axis=0, concat_axis=0, tiled=True)


def with_columns(x, circle):
    peers = lax.axis_size("lon")
    me = lax.axis_index("lon")
    lat_rows, sector, channels = x.shape
    edges = circle[:, sector:].reshape(peers, lat_rows, EDGE // lat_rows, channels)[:, :, :BAND_REACH]
    before = lax.dynamic_index_in_dim(edges, lax.rem(me + peers - 1, peers), 0, False)
    after = lax.dynamic_index_in_dim(edges, lax.rem(me + 1, peers), 0, False)
    spare = jnp.zeros((lat_rows, -(sector + 2 * BAND_REACH) % 16, channels), bf16)
    return jnp.concatenate([before, x, after, spare], axis=1)


def pairs():
    return [(i, i ^ 1) for i in range(lax.axis_size("lat"))]


def swapped_rows(x, even):
    return lax.ppermute(jnp.where(even, x[:BAND_REACH], x[1 : BAND_REACH + 1]), "lat", pairs())


def relayed_rows(far):
    peers = lax.axis_size("lat")
    relay = [(i, (i + 2) % peers if i % 2 == 0 else (i - 2) % peers) for i in range(peers)]
    return lax.ppermute(far, "lat", relay)


def rest_rows(x, even):
    return lax.ppermute(jnp.where(even, x[BAND_REACH:], x[:1]), "lat", pairs())


def on_device(states, cotangent, kernels, offsets, mixing, legendre, owner_order, spectral_gain):
    fields = states[0]
    cot = cotangent[0]
    lat_rows, sector, channels = fields.shape
    lon_index = lax.axis_index("lon")
    lat_index = lax.axis_index("lat")
    ens_index = lax.axis_index("ens")
    lon_count = lax.axis_size("lon")
    lat_count = lax.axis_size("lat")
    members = states.shape[0] * lax.axis_size("ens")
    lat_first = lat_index * lat_rows
    lat_total = lat_rows * lat_count
    kernel_number, group_count, width = mixing.shape[0], mixing.shape[1], mixing.shape[2]
    quarter = channels // lon_count
    owned, degrees = legendre.shape[0], legendre.shape[1]
    waves = owner_order.shape[0]
    main = 4 * owned
    gain_size = chunk_size(degrees // 2, lat_count)
    mix_size = chunk_size(kernel_number * width, lat_count)
    even = lat_index % 2 == 0
    blocks = WINDOWS * -(-sector // (WINDOWS * BLOCK))
    padded = blocks * BLOCK
    padded_in = padded + WINDOW - BLOCK
    sds = jax.ShapeDtypeStruct
    field_shape = sds((lat_rows, sector, channels), bf16)
    wide_shape = sds((lat_rows, padded, channels), f32)

    by_wave, by_point = wave_tables(owner_order, sector, lon_count)
    orders = lax.dynamic_slice_in_dim(owner_order, lat_index * owned, owned, 0)
    gains = lax.dynamic_slice_in_dim(spectral_gain, lon_index * quarter, quarter, 1).astype(f32)
    gains = jnp.concatenate([gains, gains], axis=1)
    leg, leg_turned = call(
        legendre_kernel,
        [sds(legendre.shape, bf16), sds((owned, lat_total, degrees), bf16)],
        (legendre,),
        4 * legendre.size * lat_total,
    )
    matrices = band_matrices(kernels, offsets, lat_first, lat_rows, lat_total)
    place = jnp.reshape(lon_index, (1,))
    parity = jnp.reshape(lat_index % 2, (1,))
    extent = lat_rows + 2 * BAND_REACH

    transform_flops = 4 * waves * LONGITUDES * lat_rows * quarter
    legendre_flops = 4 * owned * degrees * lat_total * 2 * quarter
    band_flops = 2 * blocks * matrices[0].size * channels
    row_scratch = pltpu.VMEM((4 * waves, LANES), f32)
    leg_scratch = [
        pltpu.VMEM((owned, degrees, LANES), f32),
        pltpu.VMEM(leg.shape, bf16),
        pltpu.VMEM(leg_turned.shape, bf16),
        pltpu.SemaphoreType.DMA((3, PARTS)),
    ]
    sent_shape = pltpu.HBM((lon_count, sector + EDGE, channels), bf16)
    spectrum_shape = pltpu.HBM((lon_count, sector, channels), bf16)
    tile = pl.BlockSpec((lat_rows, TILE, channels), lambda j: (0, j, 0))
    tiles = pl.cdiv(sector, TILE)

    def whole(x):
        return pl.BlockSpec(x.shape, lambda j: (0,) * x.ndim)

    def synthesized(got):
        return call(
            synthesis_kernel,
            [spectrum_shape],
            (got, by_point),
            transform_flops,
            [row_scratch, pltpu.VMEM(by_point.shape, bf16), pltpu.SemaphoreType.DMA((lon_count,))],
            places={1: pl.ANY},
        )[0]

    def band(x, far, other, which, turned):
        rest = rest_rows(x, even)
        matrix = matrices[which]
        outs = [pltpu.HBM(wide_shape.shape, f32)]
        specs = [pl.BlockSpec((lat_rows, WINDOWS * BLOCK, channels), lambda j: (0, j, 0))]
        if not turned:
            outs.append(pltpu.HBM((kernel_number, lat_rows, padded, channels), bf16))
            specs.append(
                pl.BlockSpec((kernel_number, lat_rows, WINDOWS * BLOCK, channels), lambda j: (0, 0, j, 0))
            )
        return call(
            functools.partial(band_kernel, turned),
            outs,
            (parity, hbm(x), hbm(far), hbm(rest), hbm(other), matrix, mixing),
            band_flops * 12,
            [
                pltpu.VMEM((kernel_number, channels, channels), bf16),
                pltpu.VMEM((extent, padded_in, channels), bf16),
                pltpu.SemaphoreType.DMA((4,)),
            ],
            grid=(blocks // WINDOWS,),
            blocks=[pl.BlockSpec(memory_space=SMEM)]
            + [pl.BlockSpec(memory_space=pl.ANY)] * 4
            + [whole(matrix), whole(mixing)],
            outs=specs,
        )

    (packed,) = call(pack_kernel, [sent_shape], (place, fields), 0, places={0: SMEM})
    circle = exchange(packed, "lon")
    circle, by_wave, by_point, leg, leg_turned, matrices, gains = lax.optimization_barrier(
        (circle, by_wave, by_point, leg, leg_turned, matrices, gains)
    )
    by_point, leg, leg_turned = hbm(by_point), hbm(leg), hbm(leg_turned)
    (analysed,) = call(
        analysis_kernel,
        [pltpu.HBM((lat_count, main, LANES), bf16)],
        (circle, by_wave),
        transform_flops,
        [row_scratch],
    )
    circle, analysed = lax.optimization_barrier((circle, analysed))
    extended = with_columns(fields, circle)
    far = swapped_rows(extended, even)
    owned_rows = exchange(analysed, "lat")
    synthesis, coeffs = call(
        legendre_forward_kernel,
        [pltpu.HBM((lat_count, main, LANES), bf16), pltpu.HBM((owned, degrees, LANES), f32)],
        (orders, owned_rows, leg, leg_turned, gains),
        legendre_flops,
        [row_scratch, row_scratch] + leg_scratch,
        places={0: SMEM, 2: pl.ANY, 3: pl.ANY, -2: pl.ANY},
    )
    returned = exchange(synthesis, "lat")
    other = relayed_rows(far)
    spectrum = exchange(synthesized(returned), "lon")
    mixed, basis = band(extended, far, other, 0, False)
    next_state, grad_pre, packed_back = call(
        functools.partial(activation_kernel, sector - (tiles - 1) * TILE),
        [field_shape, pltpu.HBM(field_shape.shape, bf16), sent_shape],
        (place, hbm(spectrum), hbm(mixed), hbm(fields), hbm(cot)),
        40 * fields.size,
        [pltpu.VMEM((EDGE, channels), f32)],
        grid=(tiles,),
        blocks=[pl.BlockSpec(memory_space=SMEM), tile, tile, tile, tile],
        outs=[tile, tile, tile],
    )

    circle_back = exchange(packed_back, "lon")
    (mix_part,) = call(
        mixing_gradient_kernel,
        [sds((group_count, kernel_number, width, width), f32)],
        (basis, grad_pre),
        2 * kernel_number * fields.size * width,
    )
    mix_part = mix_part.reshape(group_count, kernel_number * width, width)
    swap = [(0, 1), (1, 0)]
    kept = lax.dynamic_index_in_dim(mix_part, ens_index, 0, False)
    sent = lax.dynamic_index_in_dim(mix_part, 1 - ens_index, 0, False)
    mix_got = lax.ppermute(sent, "ens", swap)
    circle_back, kept, mix_got = lax.optimization_barrier((circle_back, kept, mix_got))
    extended_back = with_columns(grad_pre, circle_back)
    far_back = swapped_rows(extended_back, even)
    (analysed_back,) = call(
        analysis_kernel,
        [pltpu.HBM((lat_count, main + mix_size, LANES), bf16)],
        (circle_back, by_wave, hbm(kept), hbm(mix_got)),
        transform_flops,
        [row_scratch, pltpu.VMEM((2,) + kept.shape, f32), pltpu.SemaphoreType.DMA((2,))],
        places={2: pl.ANY, 3: pl.ANY},
    )
    owned_back = exchange(analysed_back, "lat")
    synthesis_back, mix_sum = call(
        legendre_backward_kernel,
        [pltpu.HBM((lat_count, main + 2 * gain_size, LANES), bf16), sds((mix_size, LANES), f32)],
        (orders, owned_back, leg, leg_turned, gains, hbm(coeffs)),
        legendre_flops,
        [row_scratch, row_scratch, pltpu.VMEM((degrees, LANES), f32)] + leg_scratch,
        places={0: SMEM, 2: pl.ANY, 3: pl.ANY, 5: pl.ANY},
    )
    returned_back = exchange(synthesis_back, "lat")
    other_back = relayed_rows(far_back)
    for bit in (1, 2):
        mix_sum += lax.ppermute(mix_sum, "lon", [(i, i ^ bit) for i in range(lon_count)])
    returned_back, other_back, mix_sum = lax.optimization_barrier((returned_back, other_back, mix_sum))
    shares = call(
        share_kernel,
        [pltpu.HBM((lat_count, 2 * (gain_size + mix_size), LANES), bf16)],
        (returned_back, mix_sum),
        0,
    )[0]
    shares = exchange(shares, "lat")
    spectrum_back = exchange(synthesized(returned_back), "lon")
    (backward,) = band(extended_back, far_back, other_back, 1, True)
    (grad_state,) = call(
        finish_kernel,
        [field_shape],
        (hbm(spectrum_back), hbm(backward), hbm(cot)),
        4 * fields.size,
        grid=(tiles,),
        blocks=[tile, tile, tile],
        outs=[tile],
    )

    mix_scale = 1.0 / math.sqrt(members * lat_total * LONGITUDES)
    gain_scale = 1.0 / math.sqrt(2 * members * degrees)
    gain_mine, mix_mine = call(
        functools.partial(collect_kernel, degrees // 2),
        [sds((degrees // 2, LANES), f32), sds((kernel_number * width, LANES), f32)],
        (shares,),
        0,
    )
    mix_other = lax.ppermute(mix_mine, "ens", swap)
    gain_other = lax.ppermute(gain_mine, "ens", swap)
    grad_mixing, grad_gain = call(
        functools.partial(totals_kernel, mix_scale, gain_scale),
        [sds(mixing.shape, f32), sds((degrees, quarter), f32)],
        (jnp.reshape(ens_index, (1,)), gain_mine, gain_other, mix_mine, mix_other),
        0,
        places={0: SMEM},
    )
    return (next_state[None], grad_state[None], grad_mixing, grad_gain)


def solution(mesh):
    in_specs = (
        P("ens", "lat", "lon", None),
        P("ens", "lat", "lon", None),
        P(),
        P(),
        P(),
        P("lat", None, None),
        P(),
        P(),
    )
    out_specs = (P("ens", "lat", "lon", None), P("ens", "lat", "lon", None), P(), P(None, "lon"))
    return jax.shard_map(
        on_device, mesh=mesh, in_specs=in_specs, out_specs=out_specs, check_vma=False
    )
```

```python
import functools
import math

import jax
import jax.numpy as jnp
from jax import lax
from jax.experimental import pallas as pl
from jax.experimental.pallas import tpu as pltpu
from jax.sharding import PartitionSpec as P

LONGITUDES = 1440
BAND_REACH = 3
SUPPORT = 4
HALF = 64
LANES = 128
BLOCK = 32
WINDOW = 48
CHUNK = 48
TILE = 96
WINDOWS = 3
EDGE = 16
PARTS = 3

bf16 = jnp.bfloat16
f32 = jnp.float32
highest = lax.Precision.HIGHEST
far_below = -1000000


VMEM = pltpu.VMEM
SMEM = pltpu.SMEM


def call(kernel, out_shape, args, flops, scratch=(), places=None, grid=(), blocks=None, outs=None, limit=24):
    moved = sum(a.size * a.dtype.itemsize for a in args)
    moved += sum(math.prod(o.shape) * jnp.dtype(o.dtype).itemsize for o in out_shape)
    places = places or {}
    specs = blocks or [pl.BlockSpec(memory_space=places.get(i, VMEM)) for i in range(len(args))]
    out_specs = outs or [
        pl.BlockSpec(memory_space=places[-1 - i]) if -1 - i in places else pl.BlockSpec()
        for i in range(len(out_shape))
    ]
    return pl.pallas_call(
        kernel,
        grid=grid,
        out_shape=out_shape,
        in_specs=specs,
        out_specs=out_specs,
        scratch_shapes=list(scratch),
        compiler_params=pltpu.CompilerParams(vmem_limit_bytes=limit * 1024 * 1024),
        cost_estimate=pl.CostEstimate(
            flops=int(flops), bytes_accessed=int(moved), transcendentals=0
        ),
    )(*args)


def hbm(x):
    return pltpu.with_memory_space_constraint(x, pltpu.HBM)


def dot(a, b):
    return lax.dot_general(a, b, (((1,), (0,)), ((), ())), preferred_element_type=f32)


def swap_pair(first, second):
    left = lax.broadcasted_iota(jnp.int32, first.shape, 1) < HALF
    low = jnp.where(left, first, pltpu.roll(second, HALF, 1))
    high = jnp.where(left, pltpu.roll(first, HALF, 1), second)
    return low, high


def quads():
    for a in range(2):
        for v in range(2):
            yield a, v, pl.ds(a * LANES, LANES), pl.ds(v * LANES, LANES)


def edge_rows(columns):
    rows = []
    for column in columns:
        rows += [column, jnp.zeros((1, column.shape[1]), f32)]
    return jnp.concatenate(rows, axis=0)


def pack_kernel(place_ref, x_ref, out_ref):
    sector = x_ref.shape[1]
    for first in range(0, sector, CHUNK):
        rows = pl.ds(first, min(CHUNK, sector - first))
        for a, v, at, av in quads():
            low, high = swap_pair(
                x_ref[2 * a, rows, av].astype(f32), x_ref[2 * a + 1, rows, av].astype(f32)
            )
            out_ref[2 * v, rows, at] = low.astype(bf16)
            out_ref[2 * v + 1, rows, at] = high.astype(bf16)
    lat_rows = x_ref.shape[0]
    begin = edge_rows([x_ref[t, 0:16, :].astype(f32)[:BAND_REACH] for t in range(lat_rows)])
    end = edge_rows([x_ref[t, sector - 8 : sector, :].astype(f32)[8 - BAND_REACH :] for t in range(lat_rows)])
    peers = out_ref.shape[0]
    for p in range(peers):
        to_right = p == lax.rem(place_ref[0] + 1, peers)
        out_ref[p, sector : sector + EDGE, :] = jnp.where(to_right, end, begin).astype(bf16)


def analysis_kernel(circle_ref, wave_ref, *rest):
    out_ref, rows_ref = rest[2:4] if len(rest) > 2 else rest
    copies = []
    if len(rest) > 2:
        terms_ref, sems = rest[4:]
        for j in range(2):
            copies.append(pltpu.make_async_copy(rest[j], terms_ref.at[j], sems.at[j]))
            copies[j].start()
    waves, sector = wave_ref.shape[1] // 2, wave_ref.shape[2]
    sums = []
    for r in range(2):
        total = None
        for s in range(wave_ref.shape[0]):
            term = dot(wave_ref[s, r * waves : (r + 1) * waves, :], circle_ref[s, 0:sector, :])
            total = term if total is None else total + term
        sums.append(total)
    for a in range(2):
        lanes = slice(a * LANES, (a + 1) * LANES)
        low, high = swap_pair(sums[0][:, lanes], sums[1][:, lanes])
        rows_ref[pl.ds(2 * a, waves, stride=4), :] = low
        rows_ref[pl.ds(2 * a + 1, waves, stride=4), :] = high
    peers = out_ref.shape[0]
    main = 4 * waves // peers
    out_ref[:, 0:main, :] = rows_ref[...].reshape(peers, main, LANES).astype(bf16)
    if copies:
        for copy in copies:
            copy.wait()
        out_ref[:, main:, :] = split_chunks(terms_ref[0] + terms_ref[1], peers)[:, 0 : out_ref.shape[1] - main, :]


def chunk_size(rows, peers):
    return 8 * -(-rows // (8 * peers))


def split_chunks(total, peers):
    high = total.astype(bf16).astype(f32)
    low = total - high
    size = chunk_size(total.shape[0], peers)
    used = total.shape[0] // size
    both = jnp.concatenate(
        [high.reshape(used, size, LANES), low.reshape(used, size, LANES)], axis=1
    )
    if used < peers:
        both = jnp.concatenate([both, jnp.zeros((peers - used, 2 * size, LANES), f32)], axis=0)
    return both.astype(bf16)


def joined(got):
    total = jnp.sum(got.astype(f32), axis=0)
    size = total.shape[0] // 2
    return total[:size] + total[size:]


def legendre_steps(order_ref, rows_in_ref, leg_ref, leg_turned_ref, gain_ref, rows_out_ref, peers, part, use):
    owned, degrees = leg_ref.shape[0], leg_ref.shape[1]
    step = 4 * owned
    degree = lax.broadcasted_iota(jnp.int32, (degrees, LANES), 0)
    for k in part:
        field = jnp.concatenate(
            [rows_in_ref[pl.ds(4 * k + t, peers, stride=step), :] for t in range(4)], axis=0
        ).astype(bf16)
        coeffs = dot(leg_ref[k], field)
        coeffs = jnp.where(degree >= order_ref[k], coeffs, 0.0)
        use(k, coeffs)
        weighted = (coeffs * gain_ref[...]).astype(bf16)
        synthesis = dot(leg_turned_ref[k], weighted)
        for t in range(4):
            rows_out_ref[pl.ds(4 * k + t, peers, stride=step), :] = synthesis[
                t * peers : (t + 1) * peers
            ]


def parts(owned):
    count = owned // PARTS
    return [(p, pl.ds(p * count, count), range(p * count, (p + 1) * count)) for p in range(PARTS)]


def legendre_forward_kernel(
    order_ref,
    got_ref,
    leg_hbm,
    leg_turned_hbm,
    gain_ref,
    out_ref,
    coeffs_hbm,
    rows_in_ref,
    rows_out_ref,
    held_ref,
    leg_ref,
    leg_turned_ref,
    sems,
):
    peers = got_ref.shape[0]
    main = rows_in_ref.shape[0] // peers
    reads, writes = [], []
    for p, at, _ in parts(leg_ref.shape[0]):
        reads.append(
            [
                pltpu.make_async_copy(leg_hbm.at[at], leg_ref.at[at], sems.at[0, p]),
                pltpu.make_async_copy(leg_turned_hbm.at[at], leg_turned_ref.at[at], sems.at[1, p]),
            ]
        )
        for copy in reads[p]:
            copy.start()
    rows_in_ref[...] = got_ref[...].astype(f32).reshape(peers * main, LANES)

    def use(k, coeffs):
        held_ref[k] = coeffs

    for p, at, part in parts(leg_ref.shape[0]):
        for copy in reads[p]:
            copy.wait()
        legendre_steps(
            order_ref, rows_in_ref, leg_ref, leg_turned_ref, gain_ref, rows_out_ref, peers, part, use
        )
        writes.append(pltpu.make_async_copy(held_ref.at[at], coeffs_hbm.at[at], sems.at[2, p]))
        writes[p].start()
    out_ref[...] = rows_out_ref[...].reshape(peers, main, LANES).astype(bf16)
    for copy in writes:
        copy.wait()


def legendre_backward_kernel(
    order_ref,
    got_ref,
    leg_hbm,
    leg_turned_hbm,
    gain_ref,
    coeffs_hbm,
    out_ref,
    mix_ref,
    rows_in_ref,
    rows_out_ref,
    sum_ref,
    held_ref,
    leg_ref,
    leg_turned_ref,
    sems,
):
    peers = got_ref.shape[0]
    main = rows_in_ref.shape[0] // peers
    reads = []
    for p, at, _ in parts(leg_ref.shape[0]):
        reads.append(
            [
                pltpu.make_async_copy(leg_hbm.at[at], leg_ref.at[at], sems.at[0, p]),
                pltpu.make_async_copy(leg_turned_hbm.at[at], leg_turned_ref.at[at], sems.at[1, p]),
                pltpu.make_async_copy(coeffs_hbm.at[at], held_ref.at[at], sems.at[2, p]),
            ]
        )
        for copy in reads[p]:
            copy.start()
    rows_in_ref[...] = got_ref[:, 0:main, :].astype(f32).reshape(peers * main, LANES)
    mix_ref[...] = jnp.sum(got_ref[:, main:, :].astype(f32), axis=0)

    def use(k, coeffs):
        term = coeffs * held_ref[k]
        if k == 0:
            sum_ref[...] = term
        else:
            sum_ref[...] += term

    for p, _, part in parts(leg_ref.shape[0]):
        for copy in reads[p]:
            copy.wait()
        legendre_steps(
            order_ref, rows_in_ref, leg_ref, leg_turned_ref, gain_ref, rows_out_ref, peers, part, use
        )
    out_ref[:, 0:main, :] = rows_out_ref[...].reshape(peers, main, LANES).astype(bf16)
    total = sum_ref[...]
    total = total + pltpu.roll(total, HALF, 1)
    half = total.shape[0] // 2
    left = lax.broadcasted_iota(jnp.int32, (half, LANES), 1) < HALF
    out_ref[:, main:, :] = split_chunks(jnp.where(left, total[:half], total[half:]), peers)


def spectrum_of(got_ref, rows_ref, waves):
    peers = got_ref.shape[0]
    main = 4 * waves // peers
    rows_ref[...] = got_ref[:, 0:main, :].astype(f32).reshape(4 * waves, LANES)
    low, high = [], []
    for a in range(2):
        lo, hi = swap_pair(
            rows_ref[pl.ds(2 * a, waves, stride=4), :], rows_ref[pl.ds(2 * a + 1, waves, stride=4), :]
        )
        low.append(lo)
        high.append(hi)
    return jnp.concatenate(
        [jnp.concatenate(low, axis=1), jnp.concatenate(high, axis=1)], axis=0
    ).astype(bf16)


def synthesis_kernel(got_ref, wave_hbm, out_ref, rows_ref, wave_ref, sems):
    peers = out_ref.shape[0]
    reads = []
    for j in range(peers):
        reads.append(pltpu.make_async_copy(wave_hbm.at[j], wave_ref.at[j], sems.at[j]))
        reads[j].start()
    spectrum = spectrum_of(got_ref, rows_ref, wave_ref.shape[2] // 2)
    for j in range(peers):
        reads[j].wait()
        out_ref[j] = dot(wave_ref[j], spectrum).astype(bf16)


def band_kernel(
    turned, parity_ref, own_hbm, far_hbm, rest_hbm, other_hbm, toeplitz_ref, mix_ref, *rest
):
    wide_ref, x_ref, sems = rest[-3:]
    mixed_ref = rest[0]
    basis_ref = rest[1] if len(rest) > 4 else None
    kernels, group_count, width = mix_ref.shape[0], mix_ref.shape[1], mix_ref.shape[2]
    span, channels = x_ref.shape[0], x_ref.shape[2]
    per_kernel = toeplitz_ref.shape[0] // kernels
    rows = per_kernel // BLOCK
    j = pl.program_id(0)

    reach, own, wide = BAND_REACH, own_hbm.shape[0], own_hbm.shape[1]

    def fetch(moves):
        copies = []
        for source, first, count in moves:
            target = x_ref.at[pl.ds(first, count), pl.ds(0, wide), :]
            copies.append(pltpu.make_async_copy(source, target, sems.at[len(copies)]))
            copies[-1].start()
        for copy in copies:
            copy.wait()

    @pl.when((j == 0) & (parity_ref[0] == 0))
    def _():
        fetch(
            [
                (own_hbm, reach, own),
                (other_hbm, 0, reach),
                (rest_hbm, reach + own, 1),
                (far_hbm.at[pl.ds(0, reach - 1)], reach + own + 1, reach - 1),
            ]
        )

    @pl.when((j == 0) & (parity_ref[0] == 1))
    def _():
        fetch(
            [
                (own_hbm, reach, own),
                (far_hbm.at[pl.ds(1, reach - 1)], 0, reach - 1),
                (rest_hbm, reach - 1, 1),
                (other_hbm, reach + own, reach),
            ]
        )

    @pl.when(j == 0)
    def _():
        x_ref[:, wide:, :] = jnp.zeros((span, x_ref.shape[1] - wide, channels), bf16)
        wide_ref[...] = jnp.zeros_like(wide_ref)
        for b in range(kernels):
            for g in range(group_count):
                part = mix_ref[b, g]
                if turned:
                    part = part.astype(f32).T.astype(bf16)
                at = slice(g * width, (g + 1) * width)
                wide_ref[b, at, at] = part

    for w in range(WINDOWS):
        start = pl.multiple_of((j * WINDOWS + w) * BLOCK, BLOCK)
        at = pl.ds(w * BLOCK, BLOCK)
        window = x_ref[:, pl.ds(start, WINDOW), :].reshape(span * WINDOW, channels)
        basis = dot(toeplitz_ref[...], window).astype(bf16)
        total = None
        for b in range(kernels):
            part = basis[b * per_kernel : (b + 1) * per_kernel]
            if basis_ref is not None:
                basis_ref[b, :, at, :] = part.reshape(rows, BLOCK, channels)
            term = dot(part, wide_ref[b])
            total = term if total is None else total + term
        mixed_ref[:, at, :] = total.reshape(rows, BLOCK, channels).astype(bf16)


def activation_kernel(
    valid, place_ref, spec_ref, mixed_ref, state_ref, cot_ref, next_ref, grad_ref, packed_ref, begin_ref
):
    scale = math.sqrt(2.0 / math.pi)
    step, steps = pl.program_id(0), pl.num_programs(0)
    lat_rows = state_ref.shape[0]
    peers = packed_ref.shape[0]
    for first in range(0, state_ref.shape[1], CHUNK):
        rows = pl.ds(first, CHUNK)
        for a, v, at, av in quads():
            spectra = swap_pair(
                spec_ref[2 * v, rows, at].astype(f32),
                spec_ref[2 * v + 1, rows, at].astype(f32),
            )
            grads = []
            for h in range(2):
                t = 2 * a + h
                value = spectra[h] + mixed_ref[t, rows, av].astype(f32)
                square = value * value
                turn = jnp.tanh(scale * value * (1.0 + 0.044715 * square))
                share = 0.5 + 0.5 * turn
                next_ref[t, rows, av] = (state_ref[t, rows, av].astype(f32) + value * share).astype(bf16)
                slope = share + (0.5 * scale) * value * (1.0 - turn * turn) * (
                    1.0 + (3.0 * 0.044715) * square
                )
                grad = cot_ref[t, rows, av].astype(f32) * slope
                grad_ref[t, rows, av] = grad.astype(bf16)
                grads.append(grad)
            low, high = swap_pair(*grads)
            packed_ref[2 * v, rows, at] = low.astype(bf16)
            packed_ref[2 * v + 1, rows, at] = high.astype(bf16)

    def edge(first, skip):
        rows = pl.ds(first, 16)
        return edge_rows(
            [grad_ref[t, rows, :].astype(f32)[skip : skip + BAND_REACH] for t in range(lat_rows)]
        )

    @pl.when(step == 0)
    def _():
        begin_ref[...] = edge(0, 0)

    @pl.when(step == steps - 1)
    def _():
        end = edge((valid - 1) // 16 * 16, (valid - 1) % 16 + 1 - BAND_REACH)
        for p in range(peers):
            to_right = p == lax.rem(place_ref[0] + 1, peers)
            packed_ref[p, valid : valid + EDGE, :] = jnp.where(to_right, end, begin_ref[...]).astype(bf16)


def finish_kernel(spec_ref, back_ref, cot_ref, out_ref):
    for first in range(0, cot_ref.shape[1], CHUNK):
        rows = pl.ds(first, CHUNK)
        for a, v, at, av in quads():
            spectra = swap_pair(
                spec_ref[2 * v, rows, at].astype(f32),
                spec_ref[2 * v + 1, rows, at].astype(f32),
            )
            for h in range(2):
                t = 2 * a + h
                out_ref[t, rows, av] = (
                    cot_ref[t, rows, av].astype(f32) + spectra[h] + back_ref[t, rows, av].astype(f32)
                ).astype(bf16)


def mixing_gradient_kernel(basis_ref, grad_ref, out_ref):
    kernels, lat_rows = basis_ref.shape[0], basis_ref.shape[1]
    sector = grad_ref.shape[1]
    for g in range(2):
        lanes = pl.ds(g * LANES, LANES)
        totals = [None] * kernels
        for i in range(lat_rows):
            turned = grad_ref[i, :, lanes].astype(f32).T.astype(bf16)
            for b in range(kernels):
                term = dot(turned, basis_ref[b, i, 0:sector, lanes])
                totals[b] = term if totals[b] is None else totals[b] + term
        for b in range(kernels):
            out_ref[g, b] = totals[b].T


def share_kernel(got_ref, mix_ref, out_ref):
    peers = got_ref.shape[0]
    gain_size = out_ref.shape[1] // 2 - mix_ref.shape[0]
    main = got_ref.shape[1] - 2 * gain_size
    total = jnp.concatenate([joined(got_ref[:, main:, :]), mix_ref[...]], axis=0)
    high = total.astype(bf16).astype(f32)
    both = jnp.concatenate([high, total - high], axis=0).astype(bf16)
    out_ref[...] = jnp.broadcast_to(both[None], out_ref.shape)


def collect_kernel(gain_rows, got_ref, gain_ref, mix_ref):
    peers, mix_rows = got_ref.shape[0], mix_ref.shape[0]
    size, mix_size = chunk_size(gain_rows, peers), chunk_size(mix_rows, peers)
    half = got_ref.shape[1] // 2
    total = got_ref[:, 0:half, :].astype(f32) + got_ref[:, half:, :].astype(f32)
    gain_ref[...] = total[0 : gain_rows // size, 0:size, :].reshape(gain_rows, LANES)
    mix_ref[...] = total[0 : mix_rows // mix_size, size:, :].reshape(mix_rows, LANES)


def totals_kernel(
    mix_scale, gain_scale, place_ref, gain_mine_ref, gain_other_ref, mine_ref, other_ref, mix_ref, gain_ref
):
    half = gain_ref.shape[0] // 2
    gain = (gain_mine_ref[...] + gain_other_ref[...]) * gain_scale
    gain_ref[0:half, :] = gain[:, 0:HALF]
    gain_ref[half:, :] = pltpu.roll(gain, HALF, 1)[:, 0:HALF]
    kernels, group_count, width = mix_ref.shape[0], mix_ref.shape[1], mix_ref.shape[2]
    for b in range(kernels):
        rows = slice(b * width, (b + 1) * width)
        mine, other = mine_ref[rows, :], other_ref[rows, :]
        for g in range(group_count):
            mix_ref[b, g] = jnp.where(place_ref[0] == g, mine, other) * mix_scale


def wave_kernel(column_ref, row_ref, cos_ref, sin_ref, by_wave_ref, by_point_ref):
    sectors, waves, sector = by_wave_ref.shape[0], cos_ref.shape[0], by_wave_ref.shape[2]
    c, s = cos_ref[...], sin_ref[...]
    for turned in range(2):
        orders = row_ref[...] if turned else column_ref[...]
        if turned:
            c, s = c.T, s.T
        for part in range(sectors):
            turns = jnp.broadcast_to((orders * part) & 3, c.shape)
            swap = (turns & 1) == 1
            flip_c = jnp.where((turns == 1) | (turns == 2), -1.0, 1.0)
            flip_s = jnp.where(turns <= 1, -1.0, 1.0)
            cos_part = (jnp.where(swap, s, c) * flip_c).astype(bf16)
            sin_part = (jnp.where(swap, c, s) * flip_s).astype(bf16)
            if turned:
                by_point_ref[part, :, 0:waves] = cos_part[0:sector]
                by_point_ref[part, :, waves : 2 * waves] = sin_part[0:sector]
            else:
                by_wave_ref[part, 0:waves, :] = cos_part[:, 0:sector]
                by_wave_ref[part, waves : 2 * waves, :] = sin_part[:, 0:sector]


def wave_tables(owner_order, sector, sectors):
    waves = owner_order.shape[0]
    n = jnp.arange(-(-sector // LANES) * LANES, dtype=jnp.int32)
    phases = owner_order[:, None] * n[None, :] % LONGITUDES
    angles = phases.astype(f32) * (2.0 * math.pi / LONGITUDES)
    factor = 1.0 / math.sqrt(LONGITUDES)
    c, s = jnp.cos(angles) * factor, jnp.sin(angles) * factor
    outs = [
        jax.ShapeDtypeStruct((sectors, 2 * waves, sector), bf16),
        jax.ShapeDtypeStruct((sectors, sector, 2 * waves), bf16),
    ]
    return call(wave_kernel, outs, (owner_order[:, None], owner_order[None, :], c, s), 30 * c.size)


def legendre_kernel(leg_ref, out_ref, turned_ref):
    owned, total = leg_ref.shape[0], leg_ref.shape[2]
    peers = total // 4
    t = lax.broadcasted_iota(jnp.int32, (total, total), 0)
    u = lax.broadcasted_iota(jnp.int32, (total, total), 1)
    order = (u == (t & 3) * peers + (t >> 2)).astype(f32).astype(bf16)
    order_turned = (t == (u & 3) * peers + (u >> 2)).astype(f32).astype(bf16)
    for k in range(owned):
        out_ref[k] = dot(leg_ref[k], order).astype(bf16)
        turned_ref[k] = lax.dot_general(
            order_turned, leg_ref[k], (((1,), (1,)), ((), ())), preferred_element_type=f32
        ).astype(bf16)


def toeplitz_kernel(table_ref, out_ref):
    outputs, entries = table_ref.shape[1], table_ref.shape[2]
    taps = 2 * BAND_REACH + 1
    shape = out_ref.shape[1:]
    entry = lax.broadcasted_iota(jnp.int32, (entries, shape[1]), 0)
    lane = lax.broadcasted_iota(jnp.int32, (1, shape[1]), 1)
    row_in = jnp.zeros_like(lane)
    for r in range(1, shape[1] // WINDOW):
        row_in += (lane >= r * WINDOW).astype(jnp.int32)
    n = lax.broadcasted_iota(jnp.int32, shape, 0) & (BLOCK - 1)
    tap = (lane - row_in * WINDOW) - n
    for which in range(2):
        tall = jnp.concatenate(
            [jnp.broadcast_to(table_ref[which, q : q + 1, :], (BLOCK, entries)) for q in range(outputs)],
            axis=0,
        ).astype(bf16)
        total = jnp.zeros(shape, f32)
        for d in range(taps):
            pick = (entry == taps * row_in + d).astype(f32).astype(bf16)
            total = jnp.where(tap == d, dot(tall, pick), total)
        out_ref[which] = total.astype(bf16)


def band_table(kernels_pad, offsets_pad, first_in, count_in, first_out, output_count):
    rows_kern = lax.dynamic_slice_in_dim(kernels_pad, first_in + BAND_REACH, count_in, 1)
    rows_start = lax.dynamic_slice_in_dim(offsets_pad, first_in + BAND_REACH, count_in, 0)
    targets = first_out + jnp.arange(output_count, dtype=jnp.int32)
    support_index = jnp.arange(SUPPORT, dtype=jnp.int32)
    matches = (
        rows_start[:, None, None] + support_index[None, :, None] == targets[None, None, :]
    ).astype(f32)
    return jnp.einsum("bikd,ikr->ibrd", rows_kern.astype(f32), matches, precision=highest)


def band_matrices(kernels, offsets, lat_first, lat_rows, lat_total):
    extent = lat_rows + 2 * BAND_REACH
    kernels_pad = jnp.pad(kernels, ((0, 0), (BAND_REACH, BAND_REACH), (0, 0), (0, 0)))
    offsets_pad = jnp.pad(offsets, BAND_REACH, constant_values=far_below)
    forward = band_table(
        kernels_pad, offsets_pad, lat_first, lat_rows, lat_first - BAND_REACH, extent
    )
    rows_global = lat_first - BAND_REACH + jnp.arange(extent, dtype=jnp.int32)
    inside = (rows_global >= 0) & (rows_global < lat_total)
    forward = jnp.where(inside[None, None, :, None], forward, 0.0)
    backward = band_table(
        kernels_pad, offsets_pad, lat_first - BAND_REACH, extent, lat_first, lat_rows
    )
    outputs, entries = kernels.shape[0] * lat_rows, extent * (2 * BAND_REACH + 1)
    tables = jnp.stack(
        [
            jnp.transpose(forward, (1, 0, 2, 3)).reshape(outputs, entries),
            jnp.transpose(backward[..., ::-1], (1, 2, 0, 3)).reshape(outputs, entries),
        ]
    )
    shape = jax.ShapeDtypeStruct((2, outputs * BLOCK, extent * WINDOW), bf16)
    return call(toeplitz_kernel, [shape], (tables,), 28 * math.prod(shape.shape))[0]


def exchange(x, axis):
    return lax.all_to_all(x, axis, split_axis=0, concat_axis=0, tiled=True)


def with_columns(x, circle):
    peers = lax.axis_size("lon")
    me = lax.axis_index("lon")
    lat_rows, sector, channels = x.shape
    edges = circle[:, sector:].reshape(peers, lat_rows, EDGE // lat_rows, channels)[:, :, :BAND_REACH]
    before = lax.dynamic_index_in_dim(edges, lax.rem(me + peers - 1, peers), 0, False)
    after = lax.dynamic_index_in_dim(edges, lax.rem(me + 1, peers), 0, False)
    spare = jnp.zeros((lat_rows, -(sector + 2 * BAND_REACH) % 16, channels), bf16)
    return jnp.concatenate([before, x, after, spare], axis=1)


def pairs():
    return [(i, i ^ 1) for i in range(lax.axis_size("lat"))]


def swapped_rows(x, even):
    return lax.ppermute(jnp.where(even, x[:BAND_REACH], x[1 : BAND_REACH + 1]), "lat", pairs())


def relayed_rows(far):
    peers = lax.axis_size("lat")
    relay = [(i, (i + 2) % peers if i % 2 == 0 else (i - 2) % peers) for i in range(peers)]
    return lax.ppermute(far, "lat", relay)


def rest_rows(x, even):
    return lax.ppermute(jnp.where(even, x[BAND_REACH:], x[:1]), "lat", pairs())


def on_device(states, cotangent, kernels, offsets, mixing, legendre, owner_order, spectral_gain):
    fields = states[0]
    cot = cotangent[0]
    lat_rows, sector, channels = fields.shape
    lon_index = lax.axis_index("lon")
    lat_index = lax.axis_index("lat")
    ens_index = lax.axis_index("ens")
    lon_count = lax.axis_size("lon")
    lat_count = lax.axis_size("lat")
    members = states.shape[0] * lax.axis_size("ens")
    lat_first = lat_index * lat_rows
    lat_total = lat_rows * lat_count
    kernel_number, group_count, width = mixing.shape[0], mixing.shape[1], mixing.shape[2]
    quarter = channels // lon_count
    owned, degrees = legendre.shape[0], legendre.shape[1]
    waves = owner_order.shape[0]
    main = 4 * owned
    gain_size = chunk_size(degrees // 2, lat_count)
    mix_size = chunk_size(kernel_number * width, lat_count)
    even = lat_index % 2 == 0
    blocks = WINDOWS * -(-sector // (WINDOWS * BLOCK))
    padded = blocks * BLOCK
    padded_in = padded + WINDOW - BLOCK
    sds = jax.ShapeDtypeStruct
    field_shape = sds((lat_rows, sector, channels), bf16)
    wide_shape = sds((lat_rows, padded, channels), f32)

    by_wave, by_point = wave_tables(owner_order, sector, lon_count)
    orders = lax.dynamic_slice_in_dim(owner_order, lat_index * owned, owned, 0)
    gains = lax.dynamic_slice_in_dim(spectral_gain, lon_index * quarter, quarter, 1).astype(f32)
    gains = jnp.concatenate([gains, gains], axis=1)
    leg, leg_turned = call(
        legendre_kernel,
        [sds(legendre.shape, bf16), sds((owned, lat_total, degrees), bf16)],
        (legendre,),
        4 * legendre.size * lat_total,
    )
    matrices = band_matrices(kernels, offsets, lat_first, lat_rows, lat_total)
    place = jnp.reshape(lon_index, (1,))
    parity = jnp.reshape(lat_index % 2, (1,))
    extent = lat_rows + 2 * BAND_REACH

    transform_flops = 4 * waves * LONGITUDES * lat_rows * quarter
    legendre_flops = 4 * owned * degrees * lat_total * 2 * quarter
    band_flops = 2 * blocks * matrices[0].size * channels
    row_scratch = pltpu.VMEM((4 * waves, LANES), f32)
    leg_scratch = [
        pltpu.VMEM((owned, degrees, LANES), f32),
        pltpu.VMEM(leg.shape, bf16),
        pltpu.VMEM(leg_turned.shape, bf16),
        pltpu.SemaphoreType.DMA((3, PARTS)),
    ]
    sent_shape = pltpu.HBM((lon_count, sector + EDGE, channels), bf16)
    spectrum_shape = pltpu.HBM((lon_count, sector, channels), bf16)
    tile = pl.BlockSpec((lat_rows, TILE, channels), lambda j: (0, j, 0))
    tiles = pl.cdiv(sector, TILE)

    def whole(x):
        return pl.BlockSpec(x.shape, lambda j: (0,) * x.ndim)

    def synthesized(got):
        return call(
            synthesis_kernel,
            [spectrum_shape],
            (got, by_point),
            transform_flops,
            [row_scratch, pltpu.VMEM(by_point.shape, bf16), pltpu.SemaphoreType.DMA((lon_count,))],
            places={1: pl.ANY},
        )[0]

    def band(x, far, other, which, turned):
        rest = rest_rows(x, even)
        matrix = matrices[which]
        outs = [pltpu.HBM(wide_shape.shape, bf16)]
        specs = [pl.BlockSpec((lat_rows, WINDOWS * BLOCK, channels), lambda j: (0, j, 0))]
        if not turned:
            outs.append(pltpu.HBM((kernel_number, lat_rows, padded, channels), bf16))
            specs.append(
                pl.BlockSpec((kernel_number, lat_rows, WINDOWS * BLOCK, channels), lambda j: (0, 0, j, 0))
            )
        return call(
            functools.partial(band_kernel, turned),
            outs,
            (parity, hbm(x), hbm(far), hbm(rest), hbm(other), matrix, mixing),
            band_flops * 12,
            [
                pltpu.VMEM((kernel_number, channels, channels), bf16),
                pltpu.VMEM((extent, padded_in, channels), bf16),
                pltpu.SemaphoreType.DMA((4,)),
            ],
            grid=(blocks // WINDOWS,),
            blocks=[pl.BlockSpec(memory_space=SMEM)]
            + [pl.BlockSpec(memory_space=pl.ANY)] * 4
            + [whole(matrix), whole(mixing)],
            outs=specs,
        )

    (packed,) = call(pack_kernel, [sent_shape], (place, fields), 0, places={0: SMEM})
    circle = exchange(packed, "lon")
    circle, by_wave, by_point, leg, leg_turned, matrices, gains = lax.optimization_barrier(
        (circle, by_wave, by_point, leg, leg_turned, matrices, gains)
    )
    by_point, leg, leg_turned = hbm(by_point), hbm(leg), hbm(leg_turned)
    (analysed,) = call(
        analysis_kernel,
        [pltpu.HBM((lat_count, main, LANES), bf16)],
        (circle, by_wave),
        transform_flops,
        [row_scratch],
    )
    circle, analysed = lax.optimization_barrier((circle, analysed))
    extended = with_columns(fields, circle)
    far = swapped_rows(extended, even)
    owned_rows = exchange(analysed, "lat")
    synthesis, coeffs = call(
        legendre_forward_kernel,
        [pltpu.HBM((lat_count, main, LANES), bf16), pltpu.HBM((owned, degrees, LANES), f32)],
        (orders, owned_rows, leg, leg_turned, gains),
        legendre_flops,
        [row_scratch, row_scratch] + leg_scratch,
        places={0: SMEM, 2: pl.ANY, 3: pl.ANY, -2: pl.ANY},
    )
    returned = exchange(synthesis, "lat")
    other = relayed_rows(far)
    spectrum = exchange(synthesized(returned), "lon")
    mixed, basis = band(extended, far, other, 0, False)
    next_state, grad_pre, packed_back = call(
        functools.partial(activation_kernel, sector - (tiles - 1) * TILE),
        [field_shape, pltpu.HBM(field_shape.shape, bf16), sent_shape],
        (place, hbm(spectrum), hbm(mixed), hbm(fields), hbm(cot)),
        40 * fields.size,
        [pltpu.VMEM((EDGE, channels), f32)],
        grid=(tiles,),
        blocks=[pl.BlockSpec(memory_space=SMEM), tile, tile, tile, tile],
        outs=[tile, tile, tile],
    )

    circle_back = exchange(packed_back, "lon")
    (mix_part,) = call(
        mixing_gradient_kernel,
        [sds((group_count, kernel_number, width, width), f32)],
        (basis, grad_pre),
        2 * kernel_number * fields.size * width,
    )
    mix_part = mix_part.reshape(group_count, kernel_number * width, width)
    swap = [(0, 1), (1, 0)]
    kept = lax.dynamic_index_in_dim(mix_part, ens_index, 0, False)
    sent = lax.dynamic_index_in_dim(mix_part, 1 - ens_index, 0, False)
    mix_got = lax.ppermute(sent, "ens", swap)
    circle_back, kept, mix_got = lax.optimization_barrier((circle_back, kept, mix_got))
    extended_back = with_columns(grad_pre, circle_back)
    far_back = swapped_rows(extended_back, even)
    (analysed_back,) = call(
        analysis_kernel,
        [pltpu.HBM((lat_count, main + mix_size, LANES), bf16)],
        (circle_back, by_wave, hbm(kept), hbm(mix_got)),
        transform_flops,
        [row_scratch, pltpu.VMEM((2,) + kept.shape, f32), pltpu.SemaphoreType.DMA((2,))],
        places={2: pl.ANY, 3: pl.ANY},
    )
    owned_back = exchange(analysed_back, "lat")
    synthesis_back, mix_sum = call(
        legendre_backward_kernel,
        [pltpu.HBM((lat_count, main + 2 * gain_size, LANES), bf16), sds((mix_size, LANES), f32)],
        (orders, owned_back, leg, leg_turned, gains, hbm(coeffs)),
        legendre_flops,
        [row_scratch, row_scratch, pltpu.VMEM((degrees, LANES), f32)] + leg_scratch,
        places={0: SMEM, 2: pl.ANY, 3: pl.ANY, 5: pl.ANY},
    )
    returned_back = exchange(synthesis_back, "lat")
    other_back = relayed_rows(far_back)
    for bit in (1, 2):
        mix_sum += lax.ppermute(mix_sum, "lon", [(i, i ^ bit) for i in range(lon_count)])
    returned_back, other_back, mix_sum = lax.optimization_barrier((returned_back, other_back, mix_sum))
    shares = call(
        share_kernel,
        [pltpu.HBM((lat_count, 2 * (gain_size + mix_size), LANES), bf16)],
        (returned_back, mix_sum),
        0,
    )[0]
    shares = exchange(shares, "lat")
    spectrum_back = exchange(synthesized(returned_back), "lon")
    (backward,) = band(extended_back, far_back, other_back, 1, True)
    (grad_state,) = call(
        finish_kernel,
        [field_shape],
        (hbm(spectrum_back), hbm(backward), hbm(cot)),
        4 * fields.size,
        grid=(tiles,),
        blocks=[tile, tile, tile],
        outs=[tile],
    )

    mix_scale = 1.0 / math.sqrt(members * lat_total * LONGITUDES)
    gain_scale = 1.0 / math.sqrt(2 * members * degrees)
    gain_mine, mix_mine = call(
        functools.partial(collect_kernel, degrees // 2),
        [sds((degrees // 2, LANES), f32), sds((kernel_number * width, LANES), f32)],
        (shares,),
        0,
    )
    mix_other = lax.ppermute(mix_mine, "ens", swap)
    gain_other = lax.ppermute(gain_mine, "ens", swap)
    grad_mixing, grad_gain = call(
        functools.partial(totals_kernel, mix_scale, gain_scale),
        [sds(mixing.shape, f32), sds((degrees, quarter), f32)],
        (jnp.reshape(ens_index, (1,)), gain_mine, gain_other, mix_mine, mix_other),
        0,
        places={0: SMEM},
    )
    return (next_state[None], grad_state[None], grad_mixing, grad_gain)


def solution(mesh):
    in_specs = (
        P("ens", "lat", "lon", None),
        P("ens", "lat", "lon", None),
        P(),
        P(),
        P(),
        P("lat", None, None),
        P(),
        P(),
    )
    out_specs = (P("ens", "lat", "lon", None), P("ens", "lat", "lon", None), P(), P(None, "lon"))
    return jax.shard_map(
        on_device, mesh=mesh, in_specs=in_specs, out_specs=out_specs, check_vma=False
    )
```
